32 devices in a mesh: groups: 2 (over y), expert: 16 (over z, x, core), dp: 1.
Axes of the slice: x: 2, y: 2, z: 4, core: 2. Of those that a mesh axis runs over, the one named last changes fastest.
Arguments:
- output_cotangent: bfloat16 [1024, 2048], P(('groups', 'expert', 'dp')), parts along dimension 0, may hold values from -6 to 6
- route: int32 [1024, 8], P(('groups', 'expert', 'dp')), parts along dimension 0, may hold values from 0 to 15, all different within a row; in each aligned block of 32 rows (0 to 31, 32 to 63, ...) at most 24 rows name the same one
- routing_weights: bfloat16 [1024, 8], P(('groups', 'expert', 'dp')), parts along dimension 0, may hold values from 0.049804688 to 1
- hidden: bfloat16 [32, 1, 16, 24, 768], P(('groups', 'expert'), 'dp'), parts along dimension 0, may hold values from -6 to 6
- down_weight: bfloat16 [16, 768, 2048], P('expert', 'dp'), may hold values from -0.21875 to 0.21875
- first_adapter_factors: bfloat16 [16, 768, 32], P('expert'), may hold values from -0.21875 to 0.21875
- second_adapter_factors: bfloat16 [16, 32, 2048], P('expert'), may hold values from -1 to 1
Outputs:
- hidden_cotangent: bfloat16 [32, 1, 16, 24, 768], P(('groups', 'expert'), 'dp'), parts along dimension 0
- first_factor_gradient: float32 [32, 768, 32], P(('groups', 'expert')), parts along dimension 0
- second_factor_gradient: float32 [32, 32, 2048], P(('groups', 'expert')), parts along dimension 0
- routing_weight_gradient: float32 [1024, 8], P(('groups', 'expert', 'dp')), parts along dimension 0
The draws below stay inside these ranges and needn't reach their ends.
There are 2 independent parts, one for each index of `groups`. The reference program is written for one: setup_inputs(seed, part) draws one part's arguments, and reference() takes and returns one part's arrays. A program takes and returns all parts, laid end to end along the dimension named above; an argument that names none is the same for every part. Nothing has to cross between parts.
Inputs may be any that keep to these rules, and one draw needn't show every extreme that they name: `route`: each row names 8 different experts. In the 32 rows of one device no expert is named by more than 24 rows, a bound that some block reaches of them.
All inputs are finite; a program needn't handle non-finite values.
Results may differ from the reference program's by a relative error of at most 0.0056.
Values may be sent and summed in bfloat16 or wider, within the bound.
No kernel may reach another device: no remote copies, remote signals or barrier semaphores. Data moves between devices by JAX's collectives and lax.ppermute only.
A program may use at most 64 MiB of HBM per device.

```python
import math
import jax
import jax.numpy as jnp
import numpy as np
from jax import lax

MODEL_SLICE = 2048
HIDDEN_SLICE = 768
ADAPTER_RANK = 32
TOPK = 8
TOK_DEV = 32
EXPERT_TOTAL = 16
TOKENS = 512
CAP = 24
N_EXPERT = 16
N_DP = 1


def shard_levels(own_key, shape, split, least, top_value):
    loudness, own = 1.0, jax.random.fold_in(own_key, 6)
    for dim, parts in split:
        heights = jnp.exp(jax.random.uniform(jax.random.fold_in(own, dim), (parts,), jnp.float32, least / len(split), top_value / len(split)))
        loudness = loudness * jnp.repeat(heights, shape[dim] // parts).reshape([-1 if axis == dim else 1 for axis in range(len(shape))])
    return loudness


def assign_block(rng, own, number, rows, number_of, top, most, lean):
    ranking = jax.random.permutation(rng, number_of)
    heavy_load, common = load_shares(number_of, rows * top, most, lean, True), load_shares(number_of, rows * top, most, lean, False)
    places = jnp.arange(number_of)

    def named(tallies, rotation):
        used = int((tallies > 0).sum())
        fixed = max(1, used // 4)
        moved = fixed + (places - fixed + rotation * (used - fixed)) % max(1, number_of - fixed)
        return jnp.zeros((number_of,), jnp.int32).at[ranking[jnp.where(places < fixed, places, moved)]].set(jnp.asarray(tallies, jnp.int32))

    tallies = jnp.where(number % 4 == 0, named(heavy_load, number // 4), named(common, number - number // 4 - 1))
    mixed = jax.random.permutation(jax.random.fold_in(own, 3), number_of)
    donor, receiver = mixed[0:number_of // 2 * 2:2], mixed[1:number_of // 2 * 2:2]
    margin = jnp.minimum(tallies[donor] - 1, most - tallies[receiver]) // 2
    margin = jnp.where((donor == ranking[0]) | (receiver == ranking[0]) | (tallies[receiver] == 0), 0, jnp.maximum(margin, 0))
    moved = jax.random.randint(jax.random.fold_in(own, 4), (number_of // 2,), 0, 1 << 20) % (margin + 1)
    tallies = tallies.at[donor].add(-moved).at[receiver].add(moved)
    labels = jnp.searchsorted(jnp.cumsum(tallies), jnp.arange(rows * top), side="right").astype(jnp.int32)
    table = labels.reshape(top, rows).T
    table = table[jax.random.permutation(jax.random.fold_in(own, 1), rows)]
    rotation = jax.random.randint(jax.random.fold_in(own, 2), (rows, 1), 0, top)
    return jnp.take_along_axis(table, (jnp.arange(top)[None, :] + rotation) % top, axis=1)


def load_shares(number_of, total, most, skew, full):
    loads = [(1 << 20) // math.isqrt(standing ** skew) + 1 for standing in range(1, number_of + 1)]
    largest = most if full else min(most, max(-(-total // number_of), total * loads[0] // sum(loads)))
    least = 1 if total - largest >= number_of - 1 else 0
    given, surplus = [largest] + [least] * (number_of - 1), total - largest - least * (number_of - 1)
    while surplus > 0:
        candidates = [i for i in range(1, number_of) if given[i] < largest] or [i for i in range(1, number_of) if given[i] < most]
        whole, budget = sum([loads[i] for i in candidates]), surplus
        for i in candidates:
            more = min(most - given[i], max(1, budget * loads[i] // whole), surplus)
            given[i] = given[i] + more
            surplus = surplus - more
    return np.array(given)


def centred(own_key, dims, width, limit, cuts=(), kind=jnp.bfloat16):
    entries = jax.random.normal(own_key, dims, jnp.float32) * width
    if len(cuts) > 0:
        entries = shard_levels(own_key, dims, cuts, -0.22, 0.18) * entries
    return jnp.clip(entries, min=-limit, max=limit).astype(kind)


def setup_inputs(seed: int = 0, part: int = 0) -> dict:
    keys = jax.random.split(jax.random.key(seed), 8)
    part_keys = jax.random.split(jax.random.fold_in(keys[7], part), 8)
    output_cotangent = centred(part_keys[0], (TOKENS, MODEL_SLICE), 1.0, 6.0, ((0, 16),))
    route_keys = jax.random.split(jax.random.fold_in(part_keys[1], 1), TOKENS // TOK_DEV)
    route_turns = jax.random.permutation(jax.random.fold_in(part_keys[1], 3), TOKENS // TOK_DEV)
    route = jax.vmap(lambda own, number: assign_block(jax.random.fold_in(part_keys[1], 2), own, number, TOK_DEV, EXPERT_TOTAL, TOPK, CAP, 2))(route_keys, route_turns).reshape((TOKENS, TOPK))
    routing_weights = jnp.clip(jnp.exp(math.log(1.0) - 2.9996462 * jax.random.uniform(part_keys[2], (TOKENS, TOPK), jnp.float32) ** shard_levels(part_keys[2], (TOKENS, TOPK), ((0, 16),), -0.2, 0.2)), 0.049804688, 1.0).astype(jnp.bfloat16)
    hidden = centred(part_keys[3], (EXPERT_TOTAL, N_DP, N_EXPERT, CAP, HIDDEN_SLICE), 1.0, 6.0, ((0, 16),))
    down_weight = centred(keys[4], (EXPERT_TOTAL, HIDDEN_SLICE, MODEL_SLICE), HIDDEN_SLICE ** -0.5, 0.21875, ((0, 16),))
    first_adapter_factors = centred(keys[5], (EXPERT_TOTAL, HIDDEN_SLICE, ADAPTER_RANK), HIDDEN_SLICE ** -0.5, 0.21875, ((0, 16),))
    second_adapter_factors = centred(keys[6], (EXPERT_TOTAL, ADAPTER_RANK, MODEL_SLICE), ADAPTER_RANK ** -0.5, 1.0, ((0, 16),))
    return dict(output_cotangent=output_cotangent, route=route, routing_weights=routing_weights, hidden=hidden, down_weight=down_weight, first_adapter_factors=first_adapter_factors, second_adapter_factors=second_adapter_factors)


adapter_scale = 2.0


def slot_positions(route):
    expert_ids = jnp.arange(EXPERT_TOTAL, dtype=jnp.int32)
    expert_hits = jnp.sum((route[:, :, None] == expert_ids[None, None, :]).astype(jnp.int32), axis=1)
    blocks = expert_hits.reshape(TOKENS // TOK_DEV, TOK_DEV, EXPERT_TOTAL)
    earlier = (jnp.cumsum(blocks, axis=1) - blocks).reshape(TOKENS, EXPERT_TOTAL)
    return jnp.take_along_axis(earlier, route, axis=1).astype(jnp.int32)


def reference(output_cotangent, route, routing_weights, hidden, down_weight, first_adapter_factors, second_adapter_factors):
    position = slot_positions(route)
    token_ids = jnp.arange(TOKENS, dtype=jnp.int32)
    source = token_ids // TOK_DEV
    source_row = jnp.broadcast_to((source // N_DP)[:, None], route.shape).astype(jnp.int32)
    source_pair = jnp.broadcast_to((source % N_DP)[:, None], route.shape).astype(jnp.int32)
    token_grid = jnp.broadcast_to(token_ids[:, None], route.shape).astype(jnp.int32)
    slot_token = jnp.full((EXPERT_TOTAL, N_DP, N_EXPERT, CAP), -1, jnp.int32)
    slot_token = slot_token.at[route, source_pair, source_row, position].set(token_grid)
    slot_weight = jnp.zeros((EXPERT_TOTAL, N_DP, N_EXPERT, CAP), jnp.bfloat16)
    slot_weight = slot_weight.at[route, source_pair, source_row, position].set(routing_weights)
    rows = N_DP * N_EXPERT * CAP

    def expert_wise(expert_slot):
        tokens_here = slot_token[expert_slot].reshape(rows)
        filled = tokens_here >= 0
        picked = output_cotangent[jnp.maximum(tokens_here, 0)]
        grad_rows = jnp.where(filled[:, None], picked, jnp.zeros_like(picked))
        weights = slot_weight[expert_slot].reshape(rows)
        hidden_inputs = hidden[expert_slot].reshape(rows, HIDDEN_SLICE)
        frozen = down_weight[expert_slot]
        first_factor = first_adapter_factors[expert_slot]
        second_factor = second_adapter_factors[expert_slot]
        reduced_rank_product = jnp.dot(hidden_inputs, first_factor, preferred_element_type=jnp.float32).astype(jnp.bfloat16)
        output_values = jnp.dot(hidden_inputs, frozen, preferred_element_type=jnp.float32)
        output_values = output_values + adapter_scale * jnp.dot(reduced_rank_product, second_factor, preferred_element_type=jnp.float32)
        slot_grad = jnp.sum(grad_rows.astype(jnp.float32) * output_values, axis=1)
        scaled_result = (weights.astype(jnp.float32)[:, None] * grad_rows.astype(jnp.float32)).astype(jnp.bfloat16)
        projected_down = jnp.dot(scaled_result, second_factor.T, preferred_element_type=jnp.float32).astype(jnp.bfloat16)
        activation_cotangent = jnp.dot(scaled_result, frozen.T, preferred_element_type=jnp.float32)
        activation_cotangent = activation_cotangent + adapter_scale * jnp.dot(projected_down, first_factor.T, preferred_element_type=jnp.float32)
        first_gradient = adapter_scale * jnp.dot(hidden_inputs.T, projected_down, preferred_element_type=jnp.float32)
        second_gradient = adapter_scale * jnp.dot(reduced_rank_product.T, scaled_result, preferred_element_type=jnp.float32)
        return (activation_cotangent.astype(jnp.bfloat16).reshape(N_DP, N_EXPERT, CAP, HIDDEN_SLICE), first_gradient, second_gradient,
                slot_grad.reshape(N_DP, N_EXPERT, CAP))

    hidden_cotangent, first_factor_gradient, second_factor_gradient, slot_gradients = lax.map(expert_wise, jnp.arange(EXPERT_TOTAL, dtype=jnp.int32))
    routing_weight_gradient = slot_gradients[route, source_pair, source_row, position]
    return hidden_cotangent, first_factor_gradient, second_factor_gradient, routing_weight_gradient
```

```python
import functools

import jax
import jax.numpy as jnp
from jax import lax
from jax.experimental import pallas as pl
from jax.experimental.pallas import tpu as pltpu
from jax.sharding import PartitionSpec as P

adapter_scale = 2.0
lanes = 128
mebibyte = 1 << 20


def slot_positions(route, expert_total):
    expert_ids = lax.broadcasted_iota(jnp.int32, (1, 1, expert_total), 2)
    expert_hits = jnp.sum((route[:, :, None] == expert_ids).astype(jnp.int32), axis=1)
    earlier = jnp.cumsum(expert_hits, axis=0) - expert_hits
    return jnp.take_along_axis(earlier, route, axis=1)


def dispatched(
    output_cotangent,
    route,
    routing_weights,
    hidden,
    down_weight,
    first_adapter_factors,
    second_adapter_factors,
):
    resident, pair_one, sources, capacity, hidden_width = hidden.shape
    expert_count = lax.axis_size("expert")
    expert_total = resident * expert_count
    model_width = output_cotangent.shape[1]
    position = slot_positions(route, expert_total)
    target = route * capacity + position
    slot_cells = lax.broadcasted_iota(jnp.int32, (expert_total * capacity, 1, 1), 0)
    matches = slot_cells == target[None, :, :]
    picker = jnp.any(matches, axis=2).astype(jnp.bfloat16)
    send_rows = jnp.dot(picker, output_cotangent, preferred_element_type=jnp.float32).astype(
        jnp.bfloat16
    )
    send_rows = send_rows.reshape(expert_total, capacity, model_width)
    send_weight = jnp.sum(
        jnp.where(matches, routing_weights[None, :, :].astype(jnp.float32), 0.0), axis=(1, 2)
    )
    send_weight = send_weight.astype(jnp.bfloat16).reshape(expert_total, capacity)
    recv_rows, recv_weight = (
        lax.all_to_all(send_rows, "expert", split_axis=0, concat_axis=0, tiled=True),
        lax.all_to_all(send_weight, "expert", split_axis=0, concat_axis=0, tiled=True),
    )
    grad_rows = recv_rows.reshape(sources, resident, capacity, model_width)
    scales = recv_weight.reshape(sources, resident, capacity)
    hidden_inputs = hidden.reshape(resident, sources, capacity, hidden_width)
    reduced_rank_product = jnp.einsum(
        "bwlv,bvs->bwls", hidden_inputs, first_adapter_factors, preferred_element_type=jnp.float32
    ).astype(jnp.bfloat16)
    adapter_result = jnp.einsum(
        "nvli,nit->vnlt",
        reduced_rank_product,
        second_adapter_factors,
        preferred_element_type=jnp.float32,
    )
    fixed_output = jnp.einsum(
        "ejcf,efd->jecd",
        hidden_inputs,
        lax.all_gather(down_weight, "dp", axis=1, tiled=True),
        preferred_element_type=jnp.float32,
    )
    output_values = fixed_output + adapter_scale * adapter_result
    slot_grad = jnp.sum(grad_rows.astype(jnp.float32) * output_values, axis=3)
    scaled_result = (scales[..., None].astype(jnp.float32) * grad_rows.astype(jnp.float32)).astype(
        jnp.bfloat16
    )
    projected_down = jnp.einsum(
        "mzxl,zil->mzxi", scaled_result, second_adapter_factors, preferred_element_type=jnp.float32
    ).astype(jnp.bfloat16)
    fixed_backward = jnp.einsum(
        "jecd,efd->ejcf",
        scaled_result,
        lax.all_gather(down_weight, "dp", axis=1, tiled=True),
        preferred_element_type=jnp.float32,
    )
    activation_cotangent = fixed_backward + adapter_scale * jnp.einsum(
        "mwsa,wqa->wmsq", projected_down, first_adapter_factors, preferred_element_type=jnp.float32
    )
    hidden_cotangent = activation_cotangent.astype(jnp.bfloat16).reshape(hidden.shape)
    first_share = adapter_scale * jnp.einsum(
        "ejcf,jecr->efr", hidden_inputs, projected_down, preferred_element_type=jnp.float32
    )
    second_share = adapter_scale * jnp.einsum(
        "ejcr,jecd->erd", reduced_rank_product, scaled_result, preferred_element_type=jnp.float32
    )
    first_factor_gradient, second_factor_gradient = lax.psum((first_share, second_share), "dp")
    returned_grads = lax.all_to_all(slot_grad, "expert", split_axis=0, concat_axis=0, tiled=True)
    returned_flat = returned_grads.reshape(expert_total * capacity)
    routing_weight_gradient = jnp.sum(jnp.where(matches, returned_flat[:, None, None], 0.0), axis=0)
    return (
        hidden_cotangent,
        first_factor_gradient,
        second_factor_gradient,
        routing_weight_gradient,
    )


def forward_kernel(hidden_ref, down_ref, first_ref, second_ref, low_ref, out_ref):
    hidden = hidden_ref[...]
    low = lax.dot_general(
        hidden, first_ref[...], (((1,), (1,)), ((), ())), preferred_element_type=jnp.float32
    ).astype(jnp.bfloat16)
    low_ref[...] = low
    width = out_ref.shape[1]
    step = min(width, 512)
    for start in range(0, width, step):
        cols = slice(start, start + step)
        out_ref[:, cols] = jnp.dot(
            hidden, down_ref[:, cols], preferred_element_type=jnp.float32
        ) + adapter_scale * jnp.dot(low, second_ref[:, cols], preferred_element_type=jnp.float32)


def combine_kernel(count, tokens, capacity, me_ref, *refs):
    blocks, (out_ref, scaled_ref, pair_ref, rows_ref, sems) = refs[:count], refs[count:]
    width = out_ref.shape[1]
    slots = count * capacity
    copies = [
        pltpu.make_async_copy(
            blocks[s], rows_ref.at[pl.ds(tokens * s, tokens), :], sems.at[s]
        )
        for s in range(count)
    ]
    for copy in copies:
        copy.start()
    for copy in copies:
        copy.wait()
    me = me_ref[0]
    hits, weights = [], []
    for s in range(count):
        meta = rows_ref[tokens * s : tokens * s + 16, width : width + lanes].astype(jnp.float32)
        match = meta[0:8] == me.astype(jnp.float32)
        hits.append(jnp.sum(jnp.where(match, 1.0, 0.0), axis=0, keepdims=True))
        weights.append(jnp.sum(jnp.where(match, meta[8:16], 0.0), axis=0, keepdims=True))
    hit = jnp.concatenate(hits, axis=0)
    weight = jnp.concatenate(weights, axis=0)
    before = (
        lax.broadcasted_iota(jnp.int32, (lanes, lanes), 0)
        < lax.broadcasted_iota(jnp.int32, (lanes, lanes), 1)
    )
    earlier = jnp.dot(
        hit.astype(jnp.bfloat16),
        jnp.where(before, 1.0, 0.0).astype(jnp.bfloat16),
        preferred_element_type=jnp.float32,
    )
    source = jnp.bitwise_xor(lax.broadcasted_iota(jnp.int32, (count, lanes), 0), me)
    target = jnp.where(hit > 0.0, (source * capacity).astype(jnp.float32) + earlier, -1.0)
    per = lanes // tokens
    lane = lax.broadcasted_iota(jnp.int32, (1, lanes), 1)
    slot = lax.broadcasted_iota(jnp.int32, (slots, lanes), 0).astype(jnp.float32)

    def merged(rows, q):
        row = rows[per * q : per * q + 1]
        for r in range(1, per):
            shifted = pltpu.roll(rows[per * q + r : per * q + r + 1], tokens * r, 1)
            row = jnp.where(lane >= tokens * r, shifted, row)
        return row

    picks, column = [], jnp.zeros((slots, 1), jnp.float32)
    for q in range(count // per):
        pick = jnp.where(slot == merged(target, q), 1.0, 0.0)
        column = column + jnp.sum(pick * merged(weight, q), axis=1, keepdims=True)
        picks.append(pick)
    picker = jnp.concatenate([pick.astype(jnp.bfloat16) for pick in picks], axis=1)
    grads = jnp.zeros((slots, 1), jnp.float32)
    step = min(width, 512)
    for start in range(0, width, step):
        cols = slice(start, start + step)
        rows = jnp.dot(picker, rows_ref[:, cols], preferred_element_type=jnp.float32)
        grads = grads + jnp.sum(rows * out_ref[:, cols], axis=1, keepdims=True)
        scaled_ref[:, cols] = (rows * column).astype(jnp.bfloat16)
    for q in range(count // per):
        row = jnp.sum(picks[q] * grads, axis=0, keepdims=True)
        for r in range(per):
            s = per * q + r
            pair_ref[s : s + 1, :] = row if r == 0 else pltpu.roll(row, lanes - tokens * r, 1)


def backward_kernel(
    scaled_ref, hidden_ref, low_ref, down_ref, first_ref, second_ref, cot_ref, dfirst_ref, dsecond_ref
):
    scaled = scaled_ref[...]
    over_last = (((1,), (1,)), ((), ()))
    over_first = (((0,), (0,)), ((), ()))
    lowered = lax.dot_general(
        scaled, second_ref[...], over_last, preferred_element_type=jnp.float32
    ).astype(jnp.bfloat16)
    fixed = lax.dot_general(scaled, down_ref[...], over_last, preferred_element_type=jnp.float32)
    adapter = jnp.dot(lowered, first_ref[...], preferred_element_type=jnp.float32)
    cot_ref[...] = (fixed + adapter_scale * adapter).astype(jnp.bfloat16)
    dfirst_ref[...] = adapter_scale * lax.dot_general(
        lowered, hidden_ref[...], over_first, preferred_element_type=jnp.float32
    )
    dsecond_ref[...] = adapter_scale * lax.dot_general(
        low_ref[...], scaled, over_first, preferred_element_type=jnp.float32
    )


vmem = pl.BlockSpec(memory_space=pltpu.VMEM)
anywhere = pl.BlockSpec(memory_space=pl.ANY)


def gathered(
    output_cotangent,
    route,
    routing_weights,
    hidden,
    down_weight,
    first_adapter_factors,
    second_adapter_factors,
):
    _, _, sources, capacity, hidden_width = hidden.shape
    tokens, width = output_cotangent.shape
    rank = first_adapter_factors.shape[2]
    count = lax.axis_size("expert")
    slots = sources * capacity
    me = lax.axis_index("expert").astype(jnp.int32)

    def swap(array, distance):
        return lax.ppermute(array, "expert", [(i, i ^ distance) for i in range(count)])

    route_rows = route.T
    meta = jnp.concatenate([route_rows.astype(jnp.bfloat16), routing_weights.T], axis=0)
    meta = jnp.pad(
        meta, ((0, tokens - meta.shape[0]), (0, lanes - tokens)), constant_values=-1.0
    )
    payload = jnp.concatenate([output_cotangent, meta], axis=1)

    hidden_rows = hidden.reshape(slots, hidden_width)
    down = down_weight[0]
    first = first_adapter_factors[0].T
    second = second_adapter_factors[0]
    low, out = pl.pallas_call(
        forward_kernel,
        out_shape=(
            jax.ShapeDtypeStruct((slots, rank), jnp.bfloat16),
            jax.ShapeDtypeStruct((slots, width), jnp.float32),
        ),
        in_specs=[vmem] * 4,
        out_specs=(vmem, vmem),
        compiler_params=pltpu.CompilerParams(vmem_limit_bytes=32 * mebibyte),
        name="forward",
    )(hidden_rows, down, first, second)

    blocks = {0: payload}
    far = [d for d in range(4, count, 4)]
    for d in far:
        blocks[d] = swap(payload, d)
    for d in [0] + far:
        blocks[d + 2] = swap(blocks[d], 2)
    for d in [0] + far:
        blocks[d + 1] = swap(blocks[d], 1)
        blocks[d + 3] = swap(blocks[d + 2], 1)

    scaled, pair = pl.pallas_call(
        functools.partial(combine_kernel, count, tokens, capacity),
        out_shape=(
            jax.ShapeDtypeStruct((slots, width), jnp.bfloat16),
            jax.ShapeDtypeStruct((count, lanes), jnp.float32),
        ),
        in_specs=[pl.BlockSpec(memory_space=pltpu.SMEM)] + [anywhere] * count + [vmem],
        out_specs=(vmem, vmem),
        scratch_shapes=[
            pltpu.VMEM((count * tokens, width + lanes), jnp.bfloat16),
            pltpu.SemaphoreType.DMA((count,)),
        ],
        compiler_params=pltpu.CompilerParams(vmem_limit_bytes=32 * mebibyte),
        name="combine",
    )(me.reshape(1), *[blocks[s] for s in range(count)], out)

    cotangent, dfirst, dsecond = pl.pallas_call(
        backward_kernel,
        out_shape=(
            jax.ShapeDtypeStruct((slots, hidden_width), jnp.bfloat16),
            jax.ShapeDtypeStruct((rank, hidden_width), jnp.float32),
            jax.ShapeDtypeStruct((rank, width), jnp.float32),
        ),
        in_specs=[vmem] * 6,
        out_specs=(vmem,) * 3,
        compiler_params=pltpu.CompilerParams(vmem_limit_bytes=32 * mebibyte),
        name="backward",
    )(scaled, hidden_rows, low, down, first, second)

    distance = lax.broadcasted_iota(jnp.int32, pair.shape, 0)
    bit = 1
    while bit < count:
        pair = jnp.where(jnp.bitwise_and(distance, bit) > 0, swap(pair, bit), pair)
        bit *= 2
    wanted = jnp.bitwise_xor(route_rows, me)[None]
    hop = lax.broadcasted_iota(jnp.int32, (count, 1, 1), 0)
    gradient = jnp.sum(jnp.where(wanted == hop, pair[:, None, :tokens], 0.0), axis=0).T
    return (
        cotangent.reshape(hidden.shape),
        dfirst.T[None],
        dsecond[None],
        gradient,
    )


def local(output_cotangent, route, routing_weights, hidden, *parameters):
    resident, pairs, sources, capacity, _ = hidden.shape
    count = lax.axis_size("expert")
    tokens, top = route.shape
    gather = (
        pairs * lax.axis_size("dp") == 1
        and resident == 1
        and count & (count - 1) == 0
        and 4 <= count <= 256
        and lanes % tokens == 0
        and count % (lanes // tokens) == 0
        and top == 8
        and 16 <= tokens <= 2 * capacity
    )
    form = gathered if gather else dispatched
    return form(output_cotangent, route, routing_weights, hidden, *parameters)


def solution(mesh):
    in_specs = (
        P(("groups", "expert", "dp"), None),
        P(("groups", "expert", "dp"), None),
        P(("groups", "expert", "dp"), None),
        P(("groups", "expert"), "dp", None, None, None),
        P("expert", "dp", None),
        P("expert", None, None),
        P("expert", None, None),
    )
    out_specs = (
        P(("groups", "expert"), "dp", None, None, None),
        P(("groups", "expert"), None, None),
        P(("groups", "expert"), None, None),
        P(("groups", "expert", "dp"), None),
    )
    return jax.shard_map(local, mesh=mesh, in_specs=in_specs, out_specs=out_specs, check_vma=False)
```

```python
import functools

import jax
import jax.numpy as jnp
from jax import lax
from jax.experimental import pallas as pl
from jax.experimental.pallas import tpu as pltpu
from jax.sharding import PartitionSpec as P

adapter_scale = 2.0
lanes = 128
mebibyte = 1 << 20
over_last = (((1,), (1,)), ((), ()))
over_first = (((0,), (0,)), ((), ()))


def slot_positions(route, expert_total):
    expert_ids = lax.broadcasted_iota(jnp.int32, (1, 1, expert_total), 2)
    expert_hits = jnp.sum((route[:, :, None] == expert_ids).astype(jnp.int32), axis=1)
    earlier = jnp.cumsum(expert_hits, axis=0) - expert_hits
    return jnp.take_along_axis(earlier, route, axis=1)


def dispatched(
    output_cotangent,
    route,
    routing_weights,
    hidden,
    down_weight,
    first_adapter_factors,
    second_adapter_factors,
):
    resident, pair_one, sources, capacity, hidden_width = hidden.shape
    expert_count = lax.axis_size("expert")
    expert_total = resident * expert_count
    model_width = output_cotangent.shape[1]
    position = slot_positions(route, expert_total)
    target = route * capacity + position
    slot_cells = lax.broadcasted_iota(jnp.int32, (expert_total * capacity, 1, 1), 0)
    matches = slot_cells == target[None, :, :]
    picker = jnp.any(matches, axis=2).astype(jnp.bfloat16)
    send_rows = jnp.dot(picker, output_cotangent, preferred_element_type=jnp.float32).astype(
        jnp.bfloat16
    )
    send_rows = send_rows.reshape(expert_total, capacity, model_width)
    send_weight = jnp.sum(
        jnp.where(matches, routing_weights[None, :, :].astype(jnp.float32), 0.0), axis=(1, 2)
    )
    send_weight = send_weight.astype(jnp.bfloat16).reshape(expert_total, capacity)
    recv_rows, recv_weight = (
        lax.all_to_all(send_rows, "expert", split_axis=0, concat_axis=0, tiled=True),
        lax.all_to_all(send_weight, "expert", split_axis=0, concat_axis=0, tiled=True),
    )
    grad_rows = recv_rows.reshape(sources, resident, capacity, model_width)
    scales = recv_weight.reshape(sources, resident, capacity)
    hidden_inputs = hidden.reshape(resident, sources, capacity, hidden_width)
    reduced_rank_product = jnp.einsum(
        "bwlv,bvs->bwls", hidden_inputs, first_adapter_factors, preferred_element_type=jnp.float32
    ).astype(jnp.bfloat16)
    adapter_result = jnp.einsum(
        "nvli,nit->vnlt",
        reduced_rank_product,
        second_adapter_factors,
        preferred_element_type=jnp.float32,
    )
    fixed_output = jnp.einsum(
        "ejcf,efd->jecd",
        hidden_inputs,
        lax.all_gather(down_weight, "dp", axis=1, tiled=True),
        preferred_element_type=jnp.float32,
    )
    output_values = fixed_output + adapter_scale * adapter_result
    slot_grad = jnp.sum(grad_rows.astype(jnp.float32) * output_values, axis=3)
    scaled_result = (scales[..., None].astype(jnp.float32) * grad_rows.astype(jnp.float32)).astype(
        jnp.bfloat16
    )
    projected_down = jnp.einsum(
        "mzxl,zil->mzxi", scaled_result, second_adapter_factors, preferred_element_type=jnp.float32
    ).astype(jnp.bfloat16)
    fixed_backward = jnp.einsum(
        "jecd,efd->ejcf",
        scaled_result,
        lax.all_gather(down_weight, "dp", axis=1, tiled=True),
        preferred_element_type=jnp.float32,
    )
    activation_cotangent = fixed_backward + adapter_scale * jnp.einsum(
        "mwsa,wqa->wmsq", projected_down, first_adapter_factors, preferred_element_type=jnp.float32
    )
    hidden_cotangent = activation_cotangent.astype(jnp.bfloat16).reshape(hidden.shape)
    first_share = adapter_scale * jnp.einsum(
        "ejcf,jecr->efr", hidden_inputs, projected_down, preferred_element_type=jnp.float32
    )
    second_share = adapter_scale * jnp.einsum(
        "ejcr,jecd->erd", reduced_rank_product, scaled_result, preferred_element_type=jnp.float32
    )
    first_factor_gradient, second_factor_gradient = lax.psum((first_share, second_share), "dp")
    returned_grads = lax.all_to_all(slot_grad, "expert", split_axis=0, concat_axis=0, tiled=True)
    returned_flat = returned_grads.reshape(expert_total * capacity)
    routing_weight_gradient = jnp.sum(jnp.where(matches, returned_flat[:, None, None], 0.0), axis=0)
    return (
        hidden_cotangent,
        first_factor_gradient,
        second_factor_gradient,
        routing_weight_gradient,
    )


def start_copies(pairs, sems):
    copies = [pltpu.make_async_copy(a, b, sems.at[i]) for i, (a, b) in enumerate(pairs)]
    for copy in copies:
        copy.start()
    return copies


def pack_kernel(
    cotangent_hbm, route_hbm, weight_hbm, payload_ref, wanted_ref, route_vmem, weight_vmem, sems
):
    tokens, width = cotangent_hbm.shape
    copies = start_copies(
        [
            (route_hbm, route_vmem),
            (weight_hbm, weight_vmem),
            (cotangent_hbm, payload_ref.at[:, pl.ds(0, width)]),
        ],
        sems,
    )
    payload_ref[:, width:] = jnp.full((tokens, lanes), -1.0, jnp.bfloat16)
    copies[0].wait()
    copies[1].wait()
    wanted_ref[...] = jnp.bitwise_xor(route_vmem[...], lax.axis_index("expert"))
    both = jnp.concatenate(
        [route_vmem[...].astype(jnp.float32), weight_vmem[...].astype(jnp.float32)], axis=0
    )
    payload_ref[:16, width : width + tokens] = both.astype(jnp.bfloat16)
    copies[2].wait()


def pieces(total, size):
    return [slice(start, start + size) for start in range(0, total, size)]


def forward_kernel(
    hidden_hbm,
    down_hbm,
    first_hbm,
    second_hbm,
    low_one,
    low_two,
    out_one,
    out_two,
    hidden,
    down,
    first,
    second,
    low,
    out,
    load_sems,
    store_sems,
):
    slots = out_one.shape[0]
    half = lax.axis_index("expert") // (lax.axis_size("expert") // 2)
    cuts = pieces(out_one.shape[1], 512)
    parts = [pl.ds(0, slots), pl.ds(slots, slots)]
    bases = [pl.multiple_of(jnp.bitwise_xor(half, part) * slots, slots) for part in (0, 1)]
    loads = start_copies(
        [(hidden_hbm.at[pl.ds(base, slots), :], hidden.at[here, :]) for base, here in zip(bases, parts)]
        + [(first_hbm, first), (second_hbm, second)]
        + [(down_hbm.at[:, cut], down.at[:, cut]) for cut in cuts],
        load_sems,
    )
    for load in loads[:3]:
        load.wait()
    low[...] = lax.dot_general(
        hidden[...], first[...], over_last, preferred_element_type=jnp.float32
    ).astype(jnp.bfloat16)
    stores = [
        pltpu.make_async_copy(low.at[here, :], low_out, store_sems.at[i])
        for i, (here, low_out) in enumerate(zip(parts, (low_one, low_two)))
    ]
    for store in stores:
        store.start()
    loads[3].wait()
    for cut, load in zip(cuts, loads[4:]):
        load.wait()
        out[:, cut] = jnp.dot(
            hidden[...], down[:, cut], preferred_element_type=jnp.float32
        ) + adapter_scale * jnp.dot(low[...], second[:, cut], preferred_element_type=jnp.float32)
        for here, out_hbm in zip(parts, (out_one, out_two)):
            store = pltpu.make_async_copy(
                out.at[here, cut], out_hbm.at[:, cut], store_sems.at[len(stores)]
            )
            store.start()
            stores.append(store)
    for store in stores:
        store.wait()


def combine(me, capacity, blocks, out_ref, scaled_ref, pair_ref, base):
    count, tokens, width = len(blocks), blocks[0].shape[0], out_ref.shape[1]
    slots = count * capacity
    hits, weights = [], []
    for block in blocks:
        meta = block[0:16, width : width + lanes].astype(jnp.float32)
        match = meta[0:8] == me.astype(jnp.float32)
        hits.append(jnp.sum(jnp.where(match, 1.0, 0.0), axis=0, keepdims=True))
        weights.append(jnp.sum(jnp.where(match, meta[8:16], 0.0), axis=0, keepdims=True))
    hit = jnp.concatenate(hits, axis=0)
    weight = jnp.concatenate(weights, axis=0)
    before = (
        lax.broadcasted_iota(jnp.int32, (lanes, lanes), 0)
        < lax.broadcasted_iota(jnp.int32, (lanes, lanes), 1)
    )
    earlier = jnp.dot(
        hit.astype(jnp.bfloat16),
        jnp.where(before, 1.0, 0.0).astype(jnp.bfloat16),
        preferred_element_type=jnp.float32,
    )
    source = jnp.bitwise_xor(lax.broadcasted_iota(jnp.int32, (count, lanes), 0), me % count)
    target = jnp.where(hit > 0.0, (source * capacity).astype(jnp.float32) + earlier, -1.0)
    per = lanes // tokens
    lane = lax.broadcasted_iota(jnp.int32, (1, lanes), 1)
    slot = lax.broadcasted_iota(jnp.int32, (slots, lanes), 0).astype(jnp.float32)

    def merged(rows, q):
        row = rows[per * q : per * q + 1]
        for r in range(1, per):
            shifted = pltpu.roll(rows[per * q + r : per * q + r + 1], tokens * r, 1)
            row = jnp.where(lane >= tokens * r, shifted, row)
        return row

    picks, column = [], jnp.zeros((slots, 1), jnp.float32)
    for q in range(count // per):
        pick = jnp.where(slot == merged(target, q), 1.0, 0.0)
        column = column + jnp.sum(pick * merged(weight, q), axis=1, keepdims=True)
        picks.append(pick)
    picker = jnp.concatenate([pick.astype(jnp.bfloat16) for pick in picks], axis=1)
    grads = jnp.zeros((slots, 1), jnp.float32)
    for cut in pieces(width, 512):
        gathered_rows = jnp.concatenate([block[:, cut] for block in blocks], axis=0)
        rows = jnp.dot(picker, gathered_rows, preferred_element_type=jnp.float32)
        grads = grads + jnp.sum(rows * out_ref[:, cut], axis=1, keepdims=True)
        scaled_ref[:, cut] = (rows * column).astype(jnp.bfloat16)
    for q in range(count // per):
        row = jnp.sum(picks[q] * grads, axis=0, keepdims=True)
        for r in range(per):
            s = base + per * q + r
            pair_ref[s : s + 1, :] = row if r == 0 else pltpu.roll(row, lanes - tokens * r, 1)


def backward(part, half, scaled_ref, low_ref, operands, outs):
    hidden_ref, down_ref, first_ref, second_ref = operands
    put_cotangent, put_first, put_second = outs
    slots = scaled_ref.shape[0]
    row_base = pl.multiple_of(jnp.bitwise_xor(half, part) * slots, slots)
    scaled = scaled_ref[...]
    lowered = lax.dot_general(
        scaled, second_ref[...], over_last, preferred_element_type=jnp.float32
    ).astype(jnp.bfloat16)
    put_second(
        adapter_scale
        * lax.dot_general(low_ref[...], scaled, over_first, preferred_element_type=jnp.float32)
    )
    put_first(
        adapter_scale
        * lax.dot_general(
            lowered,
            hidden_ref[pl.ds(row_base, slots), :],
            over_first,
            preferred_element_type=jnp.float32,
        )
    )
    fixed = lax.dot_general(scaled, down_ref[...], over_last, preferred_element_type=jnp.float32)
    adapter = jnp.dot(lowered, first_ref[...], preferred_element_type=jnp.float32)
    put_cotangent((fixed + adapter_scale * adapter).astype(jnp.bfloat16))


def first_kernel(count, capacity, *refs):
    blocks, refs = refs[:count], refs[count:]
    (out_ref, low_ref), operands, refs = refs[:2], refs[2:6], refs[6:]
    cot_ref, dfirst_ref, dsecond_ref, pair_ref, scaled_ref = refs
    me = lax.axis_index("expert")
    combine(me, capacity, blocks, out_ref, scaled_ref, pair_ref, 0)

    def put_cotangent(value):
        cot_ref[...] = value

    def put_first(value):
        dfirst_ref[...] = value

    def put_second(value):
        dsecond_ref[...] = value

    outs = put_cotangent, put_first, put_second
    backward(0, me // count, scaled_ref, low_ref, operands, outs)


def combine_kernel(count, capacity, *refs):
    blocks, (out_ref, before_ref, scaled_ref, pair_ref) = refs[:count], refs[count:]
    pair_ref[:count, :] = before_ref[...]
    combine(
        lax.axis_index("expert"), capacity, blocks, out_ref, scaled_ref, pair_ref, count
    )


def last_kernel(count, scaled_ref, low_ref, *refs):
    operands, (cot_before, dfirst_before, dsecond_before) = refs[:4], refs[4:7]
    cot_ref, dfirst_ref, dsecond_ref = refs[7:]
    half = lax.axis_index("expert") // count
    slots = scaled_ref.shape[0]
    here = pl.ds(pl.multiple_of(half * slots, slots), slots)
    there = pl.ds(pl.multiple_of((1 - half) * slots, slots), slots)
    cot_ref[here, :] = cot_before[...]

    def put_cotangent(value):
        cot_ref[there, :] = value

    def put_first(value):
        dfirst_ref[...] = value + dfirst_before[...]

    def put_second(value):
        dsecond_ref[...] = value + dsecond_before[...]

    backward(1, half, scaled_ref, low_ref, operands, (put_cotangent, put_first, put_second))


vmem = pl.BlockSpec(memory_space=pltpu.VMEM)
hbm = pl.BlockSpec(memory_space=pltpu.HBM)


def gathered(
    output_cotangent,
    route,
    routing_weights,
    hidden,
    down_weight,
    first_adapter_factors,
    second_adapter_factors,
):
    _, _, sources, capacity, hidden_width = hidden.shape
    tokens, width = output_cotangent.shape
    rank = first_adapter_factors.shape[2]
    count = lax.axis_size("expert")
    slots = sources * capacity
    half = count // 2
    bf16, f32 = jnp.bfloat16, jnp.float32

    def swap(array, distance):
        return lax.ppermute(array, "expert", [(i, i ^ distance) for i in range(count)])

    def call(limit, kernel, outs, ins, scratch, *operands, results=vmem):
        return pl.pallas_call(
            kernel,
            out_shape=tuple(jax.ShapeDtypeStruct(*out) for out in outs),
            in_specs=ins,
            out_specs=(results,) * len(outs),
            scratch_shapes=scratch,
            compiler_params=pltpu.CompilerParams(vmem_limit_bytes=limit * mebibyte),
            name=getattr(kernel, "func", kernel).__name__,
        )(*operands)

    route_rows = route.T
    payload, wanted = call(
        60,
        pack_kernel,
        [((tokens, width + lanes), bf16), (route_rows.shape, jnp.int32)],
        [hbm] * 3,
        [
            pltpu.VMEM(route_rows.shape, jnp.int32),
            pltpu.VMEM(route_rows.shape, bf16),
            pltpu.SemaphoreType.DMA((3,)),
        ],
        output_cotangent,
        route_rows,
        routing_weights.T,
    )
    hidden_rows = hidden.reshape(slots, hidden_width)
    weights = (down_weight[0], first_adapter_factors[0].T, second_adapter_factors[0])
    steps = len(pieces(width, 512))
    low, low_late, out, out_late = call(
        62,
        forward_kernel,
        [((slots // 2, rank), bf16)] * 2 + [((slots // 2, width), f32)] * 2,
        [hbm] * 4,
        [pltpu.VMEM(array.shape, bf16) for array in (hidden_rows, *weights)]
        + [pltpu.VMEM((slots, rank), bf16), pltpu.VMEM((slots, width), f32)]
        + [pltpu.SemaphoreType.DMA((4 + steps,)), pltpu.SemaphoreType.DMA((2 + 2 * steps,))],
        hidden_rows,
        *weights,
        results=hbm,
    )

    blocks = {0: payload}
    far = [d for d in range(4, count, 4)]
    near = [d for d in far if d < half]
    late = [d for d in far if d >= half]
    for d in far:
        blocks[d] = swap(payload, d)
    blocks[2] = swap(payload, 2)
    blocks[half], out, low = lax.optimization_barrier((blocks[half], out, low))
    for d in far:
        blocks[d + 2] = swap(blocks[d], 2)
    for d in [0] + near:
        blocks[d + 1] = swap(blocks[d], 1)
        blocks[d + 3] = swap(blocks[d + 2], 1)
    blocks[late[-1]], out = lax.optimization_barrier((blocks[late[-1]], out))
    grads = [((rank, hidden_width), f32), ((rank, width), f32)]
    *partial, pair = call(
        24,
        functools.partial(first_kernel, half, capacity),
        [((slots // 2, hidden_width), bf16), *grads, ((half, lanes), f32)],
        [vmem] * (half + 6),
        [pltpu.VMEM((slots // 2, width), bf16)],
        *[blocks[s] for s in range(half)],
        out,
        low,
        hidden_rows,
        *weights,
    )
    for d in late:
        blocks[d + 2], partial, pair = lax.optimization_barrier((blocks[d + 2], partial, pair))
        blocks[d + 1] = swap(blocks[d], 1)
        blocks[d + 3] = swap(blocks[d + 2], 1)
    scaled, pair = call(
        24,
        functools.partial(combine_kernel, half, capacity),
        [((slots // 2, width), bf16), ((count, lanes), f32)],
        [vmem] * (half + 2),
        [],
        *[blocks[s] for s in range(half, count)],
        out_late,
        pair,
    )
    cotangent, dfirst, dsecond = call(
        24,
        functools.partial(last_kernel, half),
        [((slots, hidden_width), bf16), *grads],
        [vmem] * 9,
        [],
        scaled,
        low_late,
        hidden_rows,
        *weights,
        *partial,
    )

    distance = lax.broadcasted_iota(jnp.int32, pair.shape, 0)
    moved = [swap(pair, d) for d in (1, 2, 3)]
    for d, values in zip((1, 2, 3), moved):
        pair = jnp.where(jnp.bitwise_and(distance, 3) == d, values, pair)
    moved = [swap(pair, d) for d in far]
    for d, values in zip(far, moved):
        pair = jnp.where(distance - jnp.bitwise_and(distance, 3) == d, values, pair)
    hop = lax.broadcasted_iota(jnp.int32, (count, 1, 1), 0)
    gradient = jnp.sum(jnp.where(wanted[None] == hop, pair[:, None, :tokens], 0.0), axis=0)
    return (
        cotangent.reshape(hidden.shape),
        dfirst.T[None],
        dsecond[None],
        gradient.T,
    )


def local(output_cotangent, route, routing_weights, hidden, *parameters):
    resident, pairs, sources, capacity, hidden_width = hidden.shape
    count = lax.axis_size("expert")
    tokens, top = route.shape
    gather = (
        pairs * lax.axis_size("dp") == 1
        and resident == 1
        and sources == count
        and count & (count - 1) == 0
        and 16 <= count <= 256
        and lanes % tokens == 0
        and (count // 2) % (lanes // tokens) == 0
        and (count // 2 * capacity) % 16 == 0
        and output_cotangent.shape[1] % 512 == 0
        and hidden_width % 256 == 0
        and top == 8
        and 16 <= tokens <= 2 * capacity
    )
    form = gathered if gather else dispatched
    return form(output_cotangent, route, routing_weights, hidden, *parameters)


def solution(mesh):
    in_specs = (
        P(("groups", "expert", "dp"), None),
        P(("groups", "expert", "dp"), None),
        P(("groups", "expert", "dp"), None),
        P(("groups", "expert"), "dp", None, None, None),
        P("expert", "dp", None),
        P("expert", None, None),
        P("expert", None, None),
    )
    out_specs = (
        P(("groups", "expert"), "dp", None, None, None),
        P(("groups", "expert"), None, None),
        P(("groups", "expert"), None, None),
        P(("groups", "expert", "dp"), None),
    )
    return jax.shard_map(local, mesh=mesh, in_specs=in_specs, out_specs=out_specs, check_vma=False)
```

```python
import functools

import jax
import jax.numpy as jnp
from jax import lax
from jax.experimental import pallas as pl
from jax.experimental.pallas import tpu as pltpu
from jax.sharding import PartitionSpec as P

adapter_scale = 2.0
lanes = 128
mebibyte = 1 << 20
over_last = (((1,), (1,)), ((), ()))
over_first = (((0,), (0,)), ((), ()))


def slot_positions(route, expert_total):
    expert_ids = lax.broadcasted_iota(jnp.int32, (1, 1, expert_total), 2)
    expert_hits = jnp.sum((route[:, :, None] == expert_ids).astype(jnp.int32), axis=1)
    earlier = jnp.cumsum(expert_hits, axis=0) - expert_hits
    return jnp.take_along_axis(earlier, route, axis=1)


def dispatched(
    output_cotangent,
    route,
    routing_weights,
    hidden,
    down_weight,
    first_adapter_factors,
    second_adapter_factors,
):
    resident, pair_one, sources, capacity, hidden_width = hidden.shape
    expert_count = lax.axis_size("expert")
    expert_total = resident * expert_count
    model_width = output_cotangent.shape[1]
    position = slot_positions(route, expert_total)
    target = route * capacity + position
    slot_cells = lax.broadcasted_iota(jnp.int32, (expert_total * capacity, 1, 1), 0)
    matches = slot_cells == target[None, :, :]
    picker = jnp.any(matches, axis=2).astype(jnp.bfloat16)
    send_rows = jnp.dot(picker, output_cotangent, preferred_element_type=jnp.float32).astype(
        jnp.bfloat16
    )
    send_rows = send_rows.reshape(expert_total, capacity, model_width)
    send_weight = jnp.sum(
        jnp.where(matches, routing_weights[None, :, :].astype(jnp.float32), 0.0), axis=(1, 2)
    )
    send_weight = send_weight.astype(jnp.bfloat16).reshape(expert_total, capacity)
    recv_rows, recv_weight = (
        lax.all_to_all(send_rows, "expert", split_axis=0, concat_axis=0, tiled=True),
        lax.all_to_all(send_weight, "expert", split_axis=0, concat_axis=0, tiled=True),
    )
    grad_rows = recv_rows.reshape(sources, resident, capacity, model_width)
    scales = recv_weight.reshape(sources, resident, capacity)
    hidden_inputs = hidden.reshape(resident, sources, capacity, hidden_width)
    reduced_rank_product = jnp.einsum(
        "bwlv,bvs->bwls", hidden_inputs, first_adapter_factors, preferred_element_type=jnp.float32
    ).astype(jnp.bfloat16)
    adapter_result = jnp.einsum(
        "nvli,nit->vnlt",
        reduced_rank_product,
        second_adapter_factors,
        preferred_element_type=jnp.float32,
    )
    fixed_output = jnp.einsum(
        "ejcf,efd->jecd",
        hidden_inputs,
        lax.all_gather(down_weight, "dp", axis=1, tiled=True),
        preferred_element_type=jnp.float32,
    )
    output_values = fixed_output + adapter_scale * adapter_result
    slot_grad = jnp.sum(grad_rows.astype(jnp.float32) * output_values, axis=3)
    scaled_result = (scales[..., None].astype(jnp.float32) * grad_rows.astype(jnp.float32)).astype(
        jnp.bfloat16
    )
    projected_down = jnp.einsum(
        "mzxl,zil->mzxi", scaled_result, second_adapter_factors, preferred_element_type=jnp.float32
    ).astype(jnp.bfloat16)
    fixed_backward = jnp.einsum(
        "jecd,efd->ejcf",
        scaled_result,
        lax.all_gather(down_weight, "dp", axis=1, tiled=True),
        preferred_element_type=jnp.float32,
    )
    activation_cotangent = fixed_backward + adapter_scale * jnp.einsum(
        "mwsa,wqa->wmsq", projected_down, first_adapter_factors, preferred_element_type=jnp.float32
    )
    hidden_cotangent = activation_cotangent.astype(jnp.bfloat16).reshape(hidden.shape)
    first_share = adapter_scale * jnp.einsum(
        "ejcf,jecr->efr", hidden_inputs, projected_down, preferred_element_type=jnp.float32
    )
    second_share = adapter_scale * jnp.einsum(
        "ejcr,jecd->erd", reduced_rank_product, scaled_result, preferred_element_type=jnp.float32
    )
    first_factor_gradient, second_factor_gradient = lax.psum((first_share, second_share), "dp")
    returned_grads = lax.all_to_all(slot_grad, "expert", split_axis=0, concat_axis=0, tiled=True)
    returned_flat = returned_grads.reshape(expert_total * capacity)
    routing_weight_gradient = jnp.sum(jnp.where(matches, returned_flat[:, None, None], 0.0), axis=0)
    return (
        hidden_cotangent,
        first_factor_gradient,
        second_factor_gradient,
        routing_weight_gradient,
    )


def start_copies(pairs, sems):
    copies = [pltpu.make_async_copy(a, b, sems.at[i]) for i, (a, b) in enumerate(pairs)]
    for copy in copies:
        copy.start()
    return copies


def pack_kernel(
    cotangent_hbm, route_hbm, weight_hbm, payload_ref, wanted_ref, route_vmem, weight_vmem, sems
):
    tokens, width = cotangent_hbm.shape
    copies = start_copies(
        [
            (route_hbm, route_vmem),
            (weight_hbm, weight_vmem),
            (cotangent_hbm, payload_ref.at[:, pl.ds(0, width)]),
        ],
        sems,
    )
    payload_ref[:, width:] = jnp.full((tokens, lanes), -1.0, jnp.bfloat16)
    copies[0].wait()
    copies[1].wait()
    wanted_ref[...] = jnp.bitwise_xor(route_vmem[...], lax.axis_index("expert"))
    both = jnp.concatenate(
        [route_vmem[...].astype(jnp.float32), weight_vmem[...].astype(jnp.float32)], axis=0
    )
    payload_ref[:16, width : width + tokens] = both.astype(jnp.bfloat16)
    copies[2].wait()


def pieces(total, size):
    return [slice(start, start + size) for start in range(0, total, size)]


def forward_kernel(
    hidden_hbm,
    down_hbm,
    first_hbm,
    second_hbm,
    low_one,
    low_two,
    out_one,
    out_two,
    hidden,
    down,
    first,
    second,
    sems,
):
    slots = out_one.shape[0]
    half = lax.axis_index("expert") // (lax.axis_size("expert") // 2)
    cuts = pieces(out_one.shape[1], 512)
    parts = [pl.ds(0, slots), pl.ds(slots, slots)]
    bases = [pl.multiple_of(jnp.bitwise_xor(half, part) * slots, slots) for part in (0, 1)]
    loads = start_copies(
        [(hidden_hbm.at[pl.ds(base, slots), :], hidden.at[here, :]) for base, here in zip(bases, parts)]
        + [(first_hbm, first), (second_hbm, second)]
        + [(down_hbm.at[:, cut], down.at[:, cut]) for cut in cuts],
        sems,
    )
    for load in loads[:3]:
        load.wait()
    low = lax.dot_general(
        hidden[...], first[...], over_last, preferred_element_type=jnp.float32
    ).astype(jnp.bfloat16)
    low_one[...] = low[:slots]
    low_two[...] = low[slots:]
    loads[3].wait()
    for cut, load in zip(cuts, loads[4:]):
        load.wait()
        values = jnp.dot(
            hidden[...], down[:, cut], preferred_element_type=jnp.float32
        ) + adapter_scale * jnp.dot(low, second[:, cut], preferred_element_type=jnp.float32)
        out_one[:, cut] = values[:slots]
        out_two[:, cut] = values[slots:]


def combine(me, capacity, blocks, out_ref, scaled_ref, pair_ref, base):
    count, tokens, width = len(blocks), blocks[0].shape[0], out_ref.shape[1]
    slots = count * capacity
    hits, weights = [], []
    for block in blocks:
        meta = block[0:16, width : width + lanes].astype(jnp.float32)
        match = meta[0:8] == me.astype(jnp.float32)
        hits.append(jnp.sum(jnp.where(match, 1.0, 0.0), axis=0, keepdims=True))
        weights.append(jnp.sum(jnp.where(match, meta[8:16], 0.0), axis=0, keepdims=True))
    hit = jnp.concatenate(hits, axis=0)
    weight = jnp.concatenate(weights, axis=0)
    before = (
        lax.broadcasted_iota(jnp.int32, (lanes, lanes), 0)
        < lax.broadcasted_iota(jnp.int32, (lanes, lanes), 1)
    )
    earlier = jnp.dot(
        hit.astype(jnp.bfloat16),
        jnp.where(before, 1.0, 0.0).astype(jnp.bfloat16),
        preferred_element_type=jnp.float32,
    )
    source = jnp.bitwise_xor(lax.broadcasted_iota(jnp.int32, (count, lanes), 0), me % count)
    target = jnp.where(hit > 0.0, (source * capacity).astype(jnp.float32) + earlier, -1.0)
    per = lanes // tokens
    lane = lax.broadcasted_iota(jnp.int32, (1, lanes), 1)
    slot = lax.broadcasted_iota(jnp.int32, (slots, lanes), 0).astype(jnp.float32)

    def merged(rows, q):
        row = rows[per * q : per * q + 1]
        for r in range(1, per):
            shifted = pltpu.roll(rows[per * q + r : per * q + r + 1], tokens * r, 1)
            row = jnp.where(lane >= tokens * r, shifted, row)
        return row

    picks, column = [], jnp.zeros((slots, 1), jnp.float32)
    for q in range(count // per):
        pick = jnp.where(slot == merged(target, q), 1.0, 0.0)
        column = column + jnp.sum(pick * merged(weight, q), axis=1, keepdims=True)
        picks.append(pick)
    picker = jnp.concatenate([pick.astype(jnp.bfloat16) for pick in picks], axis=1)
    grads = jnp.zeros((slots, 1), jnp.float32)
    for cut in pieces(width, 512):
        gathered_rows = jnp.concatenate([block[:, cut] for block in blocks], axis=0)
        rows = jnp.dot(picker, gathered_rows, preferred_element_type=jnp.float32)
        grads = grads + jnp.sum(rows * out_ref[:, cut], axis=1, keepdims=True)
        scaled_ref[:, cut] = (rows * column).astype(jnp.bfloat16)
    for q in range(count // per):
        row = jnp.sum(picks[q] * grads, axis=0, keepdims=True)
        for r in range(per):
            s = base + per * q + r
            pair_ref[s : s + 1, :] = row if r == 0 else pltpu.roll(row, lanes - tokens * r, 1)


def backward(part, scaled_ref, low_ref, operands, outs):
    hidden_ref, down_ref, first_ref, second_ref = operands
    put_cotangent, put_first, put_second = outs
    slots = scaled_ref.shape[0]
    scaled = scaled_ref[...]
    lowered = lax.dot_general(
        scaled, second_ref[...], over_last, preferred_element_type=jnp.float32
    ).astype(jnp.bfloat16)
    put_second(
        adapter_scale
        * lax.dot_general(low_ref[...], scaled, over_first, preferred_element_type=jnp.float32)
    )
    put_first(
        adapter_scale
        * lax.dot_general(
            lowered,
            hidden_ref[slots * part : slots * (part + 1), :],
            over_first,
            preferred_element_type=jnp.float32,
        )
    )
    fixed = lax.dot_general(scaled, down_ref[...], over_last, preferred_element_type=jnp.float32)
    adapter = jnp.dot(lowered, first_ref[...], preferred_element_type=jnp.float32)
    put_cotangent((fixed + adapter_scale * adapter).astype(jnp.bfloat16))


def first_kernel(count, capacity, *refs):
    blocks, refs = refs[:count], refs[count:]
    (out_ref, low_ref), operands, refs = refs[:2], refs[2:6], refs[6:]
    cot_ref, dfirst_ref, dsecond_ref, pair_ref, scaled_ref = refs
    me = lax.axis_index("expert")
    combine(me, capacity, blocks, out_ref, scaled_ref, pair_ref, 0)

    def put_cotangent(value):
        cot_ref[...] = value

    def put_first(value):
        dfirst_ref[...] = value

    def put_second(value):
        dsecond_ref[...] = value

    outs = put_cotangent, put_first, put_second
    backward(0, scaled_ref, low_ref, operands, outs)


def combine_kernel(count, capacity, *refs):
    blocks, (out_ref, before_ref, scaled_ref, pair_ref) = refs[:count], refs[count:]
    pair_ref[:count, :] = before_ref[...]
    combine(
        lax.axis_index("expert"), capacity, blocks, out_ref, scaled_ref, pair_ref, count
    )


def last_kernel(count, scaled_ref, low_ref, *refs):
    operands, (cot_before, dfirst_before, dsecond_before) = refs[:4], refs[4:7]
    cot_ref, dfirst_ref, dsecond_ref = refs[7:]
    half = lax.axis_index("expert") // count
    slots = scaled_ref.shape[0]
    here = pl.ds(pl.multiple_of(half * slots, slots), slots)
    there = pl.ds(pl.multiple_of((1 - half) * slots, slots), slots)
    cot_ref[here, :] = cot_before[...]

    def put_cotangent(value):
        cot_ref[there, :] = value

    def put_first(value):
        dfirst_ref[...] = value + dfirst_before[...]

    def put_second(value):
        dsecond_ref[...] = value + dsecond_before[...]

    backward(1, scaled_ref, low_ref, operands, (put_cotangent, put_first, put_second))


def gathered(
    output_cotangent,
    route,
    routing_weights,
    hidden,
    down_weight,
    first_adapter_factors,
    second_adapter_factors,
):
    _, _, sources, capacity, hidden_width = hidden.shape
    tokens, width = output_cotangent.shape
    rank = first_adapter_factors.shape[2]
    count = lax.axis_size("expert")
    slots = sources * capacity
    half = count // 2
    bf16, f32 = jnp.bfloat16, jnp.float32

    def swap(array, distance):
        return lax.ppermute(array, "expert", [(i, i ^ distance) for i in range(count)])

    def call(limit, kernel, outs, spaces, scratch, *operands, held_out=pltpu.VMEM):
        return pl.pallas_call(
            kernel,
            out_shape=tuple(held_out(*out) for out in outs),
            in_specs=[pl.BlockSpec(memory_space=space) for space in spaces],
            out_specs=(pl.BlockSpec(memory_space=pltpu.VMEM),) * len(outs),
            scratch_shapes=scratch,
            compiler_params=pltpu.CompilerParams(vmem_limit_bytes=limit * mebibyte),
            name=getattr(kernel, "func", kernel).__name__,
        )(*map(pltpu.with_memory_space_constraint, operands, spaces))

    route_rows = route.T
    payload, wanted = call(
        8,
        pack_kernel,
        [((tokens, width + lanes), bf16), (route_rows.shape, jnp.int32)],
        [pltpu.HBM] * 3,
        [
            pltpu.VMEM(route_rows.shape, jnp.int32),
            pltpu.VMEM(route_rows.shape, bf16),
            pltpu.SemaphoreType.DMA((3,)),
        ],
        output_cotangent,
        route_rows,
        routing_weights.T,
    )
    parameters = (
        hidden.reshape(slots, hidden_width),
        down_weight[0],
        first_adapter_factors[0].T,
        second_adapter_factors[0],
    )
    low, low_late, out, out_late, *held = call(
        24,
        forward_kernel,
        [((slots // 2, rank), bf16)] * 2
        + [((slots // 2, width), f32)] * 2
        + [(array.shape, bf16) for array in parameters],
        [pltpu.HBM] * 4,
        [pltpu.SemaphoreType.DMA((4 + len(pieces(width, 512)),))],
        *parameters,
    )

    blocks = {0: payload}
    far = [d for d in range(4, count, 4)]
    near = [d for d in far if d < half]
    late = [d for d in far if d >= half]
    for d in far:
        blocks[d] = swap(payload, d)
    blocks[2] = swap(payload, 2)
    for d in far:
        blocks[d], out, low = lax.optimization_barrier((blocks[d], out, low))
    for d in far:
        blocks[d + 2] = swap(blocks[d], 2)
    for d in [0] + near:
        blocks[d + 1] = swap(blocks[d], 1)
        blocks[d + 3] = swap(blocks[d + 2], 1)
    grads = [((rank, hidden_width), f32), ((rank, width), f32)]
    *partial, pair = call(
        24,
        functools.partial(first_kernel, half, capacity),
        [((slots // 2, hidden_width), bf16), *grads, ((half, lanes), f32)],
        [pltpu.VMEM] * (half + 6),
        [pltpu.VMEM((slots // 2, width), bf16)],
        *[blocks[s] for s in range(half)],
        out,
        low,
        *held,
    )
    for d in late:
        blocks[d + 2], partial, pair = lax.optimization_barrier((blocks[d + 2], partial, pair))
        blocks[d + 1] = swap(blocks[d], 1)
        blocks[d + 3] = swap(blocks[d + 2], 1)
    scaled, pair = call(
        24,
        functools.partial(combine_kernel, half, capacity),
        [((slots // 2, width), bf16), ((count, lanes), f32)],
        [pltpu.VMEM] * (half + 2),
        [],
        *[blocks[s] for s in range(half, count)],
        out_late,
        pair,
    )
    cotangent, dfirst, dsecond = call(
        24,
        functools.partial(last_kernel, half),
        [((slots, hidden_width), bf16), *grads],
        [pltpu.VMEM] * 9,
        [],
        scaled,
        low_late,
        *held,
        *partial,
        held_out=jax.ShapeDtypeStruct,
    )

    distance = lax.broadcasted_iota(jnp.int32, pair.shape, 0)
    moved = [swap(pair, d) for d in (1, 2, 3)]
    for d, values in zip((1, 2, 3), moved):
        pair = jnp.where(jnp.bitwise_and(distance, 3) == d, values, pair)
    pair, cotangent, dfirst, dsecond = lax.optimization_barrier(
        (pair, cotangent, dfirst, dsecond)
    )
    moved = [swap(pair, d) for d in far]
    for d, values in zip(far, moved):
        pair = jnp.where(distance - jnp.bitwise_and(distance, 3) == d, values, pair)
    hop = lax.broadcasted_iota(jnp.int32, (count, 1, 1), 0)
    gradient = jnp.sum(jnp.where(wanted[None] == hop, pair[:, None, :tokens], 0.0), axis=0)
    return (
        cotangent.reshape(hidden.shape),
        dfirst.T[None],
        dsecond[None],
        gradient.T,
    )


def local(output_cotangent, route, routing_weights, hidden, *parameters):
    resident, pairs, sources, capacity, hidden_width = hidden.shape
    count = lax.axis_size("expert")
    tokens, top = route.shape
    gather = (
        pairs * lax.axis_size("dp") == 1
        and resident == 1
        and sources == count
        and count & (count - 1) == 0
        and 16 <= count <= 256
        and lanes % tokens == 0
        and (count // 2) % (lanes // tokens) == 0
        and (count // 2 * capacity) % 16 == 0
        and output_cotangent.shape[1] % 512 == 0
        and hidden_width % 256 == 0
        and top == 8
        and 16 <= tokens <= 2 * capacity
    )
    form = gathered if gather else dispatched
    return form(output_cotangent, route, routing_weights, hidden, *parameters)


def solution(mesh):
    in_specs = (
        P(("groups", "expert", "dp"), None),
        P(("groups", "expert", "dp"), None),
        P(("groups", "expert", "dp"), None),
        P(("groups", "expert"), "dp", None, None, None),
        P("expert", "dp", None),
        P("expert", None, None),
        P("expert", None, None),
    )
    out_specs = (
        P(("groups", "expert"), "dp", None, None, None),
        P(("groups", "expert"), None, None),
        P(("groups", "expert"), None, None),
        P(("groups", "expert", "dp"), None),
    )
    return jax.shard_map(local, mesh=mesh, in_specs=in_specs, out_specs=out_specs, check_vma=False)
```

```python
import functools

import jax
import jax.numpy as jnp
from jax import lax
from jax.experimental import pallas as pl
from jax.experimental.pallas import tpu as pltpu
from jax.sharding import PartitionSpec as P

adapter_scale = 2.0
lanes = 128
mebibyte = 1 << 20
over_last = (((1,), (1,)), ((), ()))
over_first = (((0,), (0,)), ((), ()))


def slot_positions(route, expert_total):
    expert_ids = lax.broadcasted_iota(jnp.int32, (1, 1, expert_total), 2)
    expert_hits = jnp.sum((route[:, :, None] == expert_ids).astype(jnp.int32), axis=1)
    earlier = jnp.cumsum(expert_hits, axis=0) - expert_hits
    return jnp.take_along_axis(earlier, route, axis=1)


def dispatched(
    output_cotangent,
    route,
    routing_weights,
    hidden,
    down_weight,
    first_adapter_factors,
    second_adapter_factors,
):
    resident, pair_one, sources, capacity, hidden_width = hidden.shape
    expert_count = lax.axis_size("expert")
    expert_total = resident * expert_count
    model_width = output_cotangent.shape[1]
    position = slot_positions(route, expert_total)
    target = route * capacity + position
    slot_cells = lax.broadcasted_iota(jnp.int32, (expert_total * capacity, 1, 1), 0)
    matches = slot_cells == target[None, :, :]
    picker = jnp.any(matches, axis=2).astype(jnp.bfloat16)
    send_rows = jnp.dot(picker, output_cotangent, preferred_element_type=jnp.float32).astype(
        jnp.bfloat16
    )
    send_rows = send_rows.reshape(expert_total, capacity, model_width)
    send_weight = jnp.sum(
        jnp.where(matches, routing_weights[None, :, :].astype(jnp.float32), 0.0), axis=(1, 2)
    )
    send_weight = send_weight.astype(jnp.bfloat16).reshape(expert_total, capacity)
    recv_rows, recv_weight = (
        lax.all_to_all(send_rows, "expert", split_axis=0, concat_axis=0, tiled=True),
        lax.all_to_all(send_weight, "expert", split_axis=0, concat_axis=0, tiled=True),
    )
    grad_rows = recv_rows.reshape(sources, resident, capacity, model_width)
    scales = recv_weight.reshape(sources, resident, capacity)
    hidden_inputs = hidden.reshape(resident, sources, capacity, hidden_width)
    reduced_rank_product = jnp.einsum(
        "bwlv,bvs->bwls", hidden_inputs, first_adapter_factors, preferred_element_type=jnp.float32
    ).astype(jnp.bfloat16)
    adapter_result = jnp.einsum(
        "nvli,nit->vnlt",
        reduced_rank_product,
        second_adapter_factors,
        preferred_element_type=jnp.float32,
    )
    fixed_output = jnp.einsum(
        "ejcf,efd->jecd",
        hidden_inputs,
        lax.all_gather(down_weight, "dp", axis=1, tiled=True),
        preferred_element_type=jnp.float32,
    )
    output_values = fixed_output + adapter_scale * adapter_result
    slot_grad = jnp.sum(grad_rows.astype(jnp.float32) * output_values, axis=3)
    scaled_result = (scales[..., None].astype(jnp.float32) * grad_rows.astype(jnp.float32)).astype(
        jnp.bfloat16
    )
    projected_down = jnp.einsum(
        "mzxl,zil->mzxi", scaled_result, second_adapter_factors, preferred_element_type=jnp.float32
    ).astype(jnp.bfloat16)
    fixed_backward = jnp.einsum(
        "jecd,efd->ejcf",
        scaled_result,
        lax.all_gather(down_weight, "dp", axis=1, tiled=True),
        preferred_element_type=jnp.float32,
    )
    activation_cotangent = fixed_backward + adapter_scale * jnp.einsum(
        "mwsa,wqa->wmsq", projected_down, first_adapter_factors, preferred_element_type=jnp.float32
    )
    hidden_cotangent = activation_cotangent.astype(jnp.bfloat16).reshape(hidden.shape)
    first_share = adapter_scale * jnp.einsum(
        "ejcf,jecr->efr", hidden_inputs, projected_down, preferred_element_type=jnp.float32
    )
    second_share = adapter_scale * jnp.einsum(
        "ejcr,jecd->erd", reduced_rank_product, scaled_result, preferred_element_type=jnp.float32
    )
    first_factor_gradient, second_factor_gradient = lax.psum((first_share, second_share), "dp")
    returned_grads = lax.all_to_all(slot_grad, "expert", split_axis=0, concat_axis=0, tiled=True)
    returned_flat = returned_grads.reshape(expert_total * capacity)
    routing_weight_gradient = jnp.sum(jnp.where(matches, returned_flat[:, None, None], 0.0), axis=0)
    return (
        hidden_cotangent,
        first_factor_gradient,
        second_factor_gradient,
        routing_weight_gradient,
    )


def start_copies(pairs, sems):
    copies = [pltpu.make_async_copy(a, b, sems.at[i]) for i, (a, b) in enumerate(pairs)]
    for copy in copies:
        copy.start()
    return copies


def pack_kernel(
    cotangent_hbm, route_hbm, weight_hbm, payload_ref, wanted_ref, route_vmem, weight_vmem, sems
):
    tokens, width = cotangent_hbm.shape
    copies = start_copies(
        [
            (route_hbm, route_vmem),
            (weight_hbm, weight_vmem),
            (cotangent_hbm, payload_ref.at[:, pl.ds(0, width)]),
        ],
        sems,
    )
    payload_ref[:, width:] = jnp.full((tokens, lanes), -1.0, jnp.bfloat16)
    copies[0].wait()
    copies[1].wait()
    wanted_ref[...] = jnp.bitwise_xor(route_vmem[...], lax.axis_index("expert"))
    both = jnp.concatenate(
        [route_vmem[...].astype(jnp.float32), weight_vmem[...].astype(jnp.float32)], axis=0
    )
    payload_ref[:16, width : width + tokens] = both.astype(jnp.bfloat16)
    copies[2].wait()


def pieces(total, size):
    return [slice(start, start + size) for start in range(0, total, size)]


def load_kernel(hidden_hbm, down_hbm, first_hbm, second_hbm, *refs):
    (hidden, down, first, second), sems = refs[:4], refs[4]
    slots = hidden.shape[0] // 2
    half = lax.axis_index("expert") // (lax.axis_size("expert") // 2)
    pairs = [(down_hbm, down), (first_hbm, first), (second_hbm, second)]
    for part in (0, 1):
        base = pl.multiple_of(jnp.bitwise_xor(half, part) * slots, slots)
        pairs.append((hidden_hbm.at[pl.ds(base, slots), :], hidden.at[pl.ds(slots * part, slots), :]))
    for copy in start_copies(pairs, sems):
        copy.wait()


def forward_kernel(
    hidden, down, first, second, low_one, low_two, out_one, out_two
):
    slots = out_one.shape[0]
    low = lax.dot_general(
        hidden[...], first[...], over_last, preferred_element_type=jnp.float32
    ).astype(jnp.bfloat16)
    low_one[...] = low[:slots]
    low_two[...] = low[slots:]
    for cut in pieces(out_one.shape[1], 512):
        values = jnp.dot(
            hidden[...], down[:, cut], preferred_element_type=jnp.float32
        ) + adapter_scale * jnp.dot(low, second[:, cut], preferred_element_type=jnp.float32)
        out_one[:, cut] = values[:slots]
        out_two[:, cut] = values[slots:]


def combine(me, capacity, blocks, out_ref, scaled_ref, pair_ref, base):
    count, tokens, width = len(blocks), blocks[0].shape[0], out_ref.shape[1]
    slots = count * capacity
    hits, weights = [], []
    for block in blocks:
        meta = block[0:16, width : width + lanes].astype(jnp.float32)
        match = meta[0:8] == me.astype(jnp.float32)
        hits.append(jnp.sum(jnp.where(match, 1.0, 0.0), axis=0, keepdims=True))
        weights.append(jnp.sum(jnp.where(match, meta[8:16], 0.0), axis=0, keepdims=True))
    hit = jnp.concatenate(hits, axis=0)
    weight = jnp.concatenate(weights, axis=0)
    before = (
        lax.broadcasted_iota(jnp.int32, (lanes, lanes), 0)
        < lax.broadcasted_iota(jnp.int32, (lanes, lanes), 1)
    )
    earlier = jnp.dot(
        hit.astype(jnp.bfloat16),
        jnp.where(before, 1.0, 0.0).astype(jnp.bfloat16),
        preferred_element_type=jnp.float32,
    )
    source = jnp.bitwise_xor(lax.broadcasted_iota(jnp.int32, (count, lanes), 0), me % count)
    target = jnp.where(hit > 0.0, (source * capacity).astype(jnp.float32) + earlier, -1.0)
    per = lanes // tokens
    lane = lax.broadcasted_iota(jnp.int32, (1, lanes), 1)
    slot = lax.broadcasted_iota(jnp.int32, (slots, lanes), 0).astype(jnp.float32)

    def merged(rows, q):
        row = rows[per * q : per * q + 1]
        for r in range(1, per):
            shifted = pltpu.roll(rows[per * q + r : per * q + r + 1], tokens * r, 1)
            row = jnp.where(lane >= tokens * r, shifted, row)
        return row

    picks, column = [], jnp.zeros((slots, 1), jnp.float32)
    for q in range(count // per):
        pick = jnp.where(slot == merged(target, q), 1.0, 0.0)
        column = column + jnp.sum(pick * merged(weight, q), axis=1, keepdims=True)
        picks.append(pick)
    picker = jnp.concatenate([pick.astype(jnp.bfloat16) for pick in picks], axis=1)
    grads = jnp.zeros((slots, 1), jnp.float32)
    for cut in pieces(width, 512):
        gathered_rows = jnp.concatenate([block[:, cut] for block in blocks], axis=0)
        rows = jnp.dot(picker, gathered_rows, preferred_element_type=jnp.float32)
        grads = grads + jnp.sum(rows * out_ref[:, cut], axis=1, keepdims=True)
        scaled_ref[:, cut] = (rows * column).astype(jnp.bfloat16)
    for q in range(count // per):
        row = jnp.sum(picks[q] * grads, axis=0, keepdims=True)
        for r in range(per):
            s = base + per * q + r
            pair_ref[s : s + 1, :] = row if r == 0 else pltpu.roll(row, lanes - tokens * r, 1)


def backward(part, scaled_ref, low_ref, operands, outs):
    hidden_ref, down_ref, first_ref, second_ref = operands
    put_cotangent, put_first, put_second = outs
    slots = scaled_ref.shape[0]
    scaled = scaled_ref[...]
    lowered = lax.dot_general(
        scaled, second_ref[...], over_last, preferred_element_type=jnp.float32
    ).astype(jnp.bfloat16)
    put_second(
        adapter_scale
        * lax.dot_general(low_ref[...], scaled, over_first, preferred_element_type=jnp.float32)
    )
    put_first(
        adapter_scale
        * lax.dot_general(
            lowered,
            hidden_ref[slots * part : slots * (part + 1), :],
            over_first,
            preferred_element_type=jnp.float32,
        )
    )
    fixed = lax.dot_general(scaled, down_ref[...], over_last, preferred_element_type=jnp.float32)
    adapter = jnp.dot(lowered, first_ref[...], preferred_element_type=jnp.float32)
    put_cotangent((fixed + adapter_scale * adapter).astype(jnp.bfloat16))


def first_kernel(count, capacity, *refs):
    blocks, refs = refs[:count], refs[count:]
    (out_ref, low_ref), operands, refs = refs[:2], refs[2:6], refs[6:]
    cot_ref, dfirst_ref, dsecond_ref, pair_ref, scaled_ref = refs
    me = lax.axis_index("expert")
    combine(me, capacity, blocks, out_ref, scaled_ref, pair_ref, 0)

    def put_cotangent(value):
        cot_ref[...] = value

    def put_first(value):
        dfirst_ref[...] = value

    def put_second(value):
        dsecond_ref[...] = value

    outs = put_cotangent, put_first, put_second
    backward(0, scaled_ref, low_ref, operands, outs)


def combine_kernel(count, capacity, *refs):
    blocks, (out_ref, before_ref, scaled_ref, pair_ref) = refs[:count], refs[count:]
    pair_ref[:count, :] = before_ref[...]
    combine(
        lax.axis_index("expert"), capacity, blocks, out_ref, scaled_ref, pair_ref, count
    )


def last_kernel(count, scaled_ref, low_ref, *refs):
    operands, (cot_before, dfirst_before, dsecond_before) = refs[:4], refs[4:7]
    cot_ref, dfirst_ref, dsecond_ref = refs[7:]
    half = lax.axis_index("expert") // count
    slots = scaled_ref.shape[0]
    here = pl.ds(pl.multiple_of(half * slots, slots), slots)
    there = pl.ds(pl.multiple_of((1 - half) * slots, slots), slots)
    cot_ref[here, :] = cot_before[...]

    def put_cotangent(value):
        cot_ref[there, :] = value

    def put_first(value):
        dfirst_ref[...] = value + dfirst_before[...]

    def put_second(value):
        dsecond_ref[...] = value + dsecond_before[...]

    backward(1, scaled_ref, low_ref, operands, (put_cotangent, put_first, put_second))


def gathered(
    output_cotangent,
    route,
    routing_weights,
    hidden,
    down_weight,
    first_adapter_factors,
    second_adapter_factors,
):
    _, _, sources, capacity, hidden_width = hidden.shape
    tokens, width = output_cotangent.shape
    rank = first_adapter_factors.shape[2]
    count = lax.axis_size("expert")
    slots = sources * capacity
    half = count // 2
    bf16, f32 = jnp.bfloat16, jnp.float32

    def swap(array, distance):
        return lax.ppermute(array, "expert", [(i, i ^ distance) for i in range(count)])

    def call(limit, kernel, outs, spaces, scratch, *operands, held_out=pltpu.VMEM):
        return pl.pallas_call(
            kernel,
            out_shape=tuple(held_out(*out) for out in outs),
            in_specs=[pl.BlockSpec(memory_space=space) for space in spaces],
            out_specs=(pl.BlockSpec(memory_space=pltpu.VMEM),) * len(outs),
            scratch_shapes=scratch,
            compiler_params=pltpu.CompilerParams(vmem_limit_bytes=limit * mebibyte),
            name=getattr(kernel, "func", kernel).__name__,
        )(*map(pltpu.with_memory_space_constraint, operands, spaces))

    route_rows = route.T
    payload, wanted = call(
        8,
        pack_kernel,
        [((tokens, width + lanes), bf16), (route_rows.shape, jnp.int32)],
        [pltpu.HBM] * 3,
        [
            pltpu.VMEM(route_rows.shape, jnp.int32),
            pltpu.VMEM(route_rows.shape, bf16),
            pltpu.SemaphoreType.DMA((3,)),
        ],
        output_cotangent,
        route_rows,
        routing_weights.T,
    )
    blocks = {0: payload}
    far = [d for d in range(4, count, 4)]
    near = [d for d in far if d < half]
    late = [d for d in far if d >= half]
    direct = [d for d in far if d & (d - 1) == 0]
    for d in direct[::-1]:
        blocks[d] = swap(payload, d)
    blocks[2] = swap(payload, 2)
    parameters = (
        hidden.reshape(slots, hidden_width),
        down_weight[0],
        first_adapter_factors[0].T,
        second_adapter_factors[0],
    )
    held = call(
        8,
        load_kernel,
        [(array.shape, bf16) for array in parameters],
        [pltpu.HBM] * 4,
        [pltpu.SemaphoreType.DMA((5,))],
        *parameters,
    )
    blocks[near[0]], held = lax.optimization_barrier((blocks[near[0]], held))
    low, low_late, out, out_late = call(
        24,
        forward_kernel,
        [((slots // 2, rank), bf16)] * 2 + [((slots // 2, width), f32)] * 2,
        [pltpu.VMEM] * 4,
        [],
        *held,
    )

    for d in far:
        if d not in direct:
            blocks[d] = swap(blocks[half], d - half)
    for d in far:
        blocks[d + 2] = swap(blocks[d], 2)
    for d in [0] + near:
        blocks[d + 1] = swap(blocks[d], 1)
        blocks[d + 3] = swap(blocks[d + 2], 1)
    grads = [((rank, hidden_width), f32), ((rank, width), f32)]
    *partial, pair = call(
        24,
        functools.partial(first_kernel, half, capacity),
        [((slots // 2, hidden_width), bf16), *grads, ((half, lanes), f32)],
        [pltpu.VMEM] * (half + 6),
        [pltpu.VMEM((slots // 2, width), bf16)],
        *[blocks[s] for s in range(half)],
        out,
        low,
        *held,
    )
    for d in late:
        blocks[d + 2], partial, pair = lax.optimization_barrier((blocks[d + 2], partial, pair))
        blocks[d + 1] = swap(blocks[d], 1)
        blocks[d + 3] = swap(blocks[d + 2], 1)
    scaled, pair = call(
        24,
        functools.partial(combine_kernel, half, capacity),
        [((slots // 2, width), bf16), ((count, lanes), f32)],
        [pltpu.VMEM] * (half + 2),
        [],
        *[blocks[s] for s in range(half, count)],
        out_late,
        pair,
    )
    cotangent, dfirst, dsecond = call(
        24,
        functools.partial(last_kernel, half),
        [((slots, hidden_width), bf16), *grads],
        [pltpu.VMEM] * 9,
        [],
        scaled,
        low_late,
        *held,
        *partial,
        held_out=jax.ShapeDtypeStruct,
    )

    distance = lax.broadcasted_iota(jnp.int32, pair.shape, 0)
    moved = [swap(pair, d) for d in far]
    for d, values in zip(far, moved):
        pair = jnp.where(distance - jnp.bitwise_and(distance, 3) == d, values, pair)
    pair, cotangent, dfirst, dsecond = lax.optimization_barrier(
        (pair, cotangent, dfirst, dsecond)
    )
    moved = [swap(pair, d) for d in (1, 2, 3)]
    for d, values in zip((1, 2, 3), moved):
        pair = jnp.where(jnp.bitwise_and(distance, 3) == d, values, pair)
    hop = lax.broadcasted_iota(jnp.int32, (count, 1, 1), 0)
    gradient = jnp.sum(jnp.where(wanted[None] == hop, pair[:, None, :tokens], 0.0), axis=0)
    return (
        cotangent.reshape(hidden.shape),
        dfirst.T[None],
        dsecond[None],
        gradient.T,
    )


def local(output_cotangent, route, routing_weights, hidden, *parameters):
    resident, pairs, sources, capacity, hidden_width = hidden.shape
    count = lax.axis_size("expert")
    tokens, top = route.shape
    gather = (
        pairs * lax.axis_size("dp") == 1
        and resident == 1
        and sources == count
        and count & (count - 1) == 0
        and 16 <= count <= 256
        and lanes % tokens == 0
        and (count // 2) % (lanes // tokens) == 0
        and (count // 2 * capacity) % 16 == 0
        and output_cotangent.shape[1] % 512 == 0
        and hidden_width % 256 == 0
        and top == 8
        and 16 <= tokens <= 2 * capacity
    )
    form = gathered if gather else dispatched
    return form(output_cotangent, route, routing_weights, hidden, *parameters)


def solution(mesh):
    in_specs = (
        P(("groups", "expert", "dp"), None),
        P(("groups", "expert", "dp"), None),
        P(("groups", "expert", "dp"), None),
        P(("groups", "expert"), "dp", None, None, None),
        P("expert", "dp", None),
        P("expert", None, None),
        P("expert", None, None),
    )
    out_specs = (
        P(("groups", "expert"), "dp", None, None, None),
        P(("groups", "expert"), None, None),
        P(("groups", "expert"), None, None),
        P(("groups", "expert", "dp"), None),
    )
    return jax.shard_map(local, mesh=mesh, in_specs=in_specs, out_specs=out_specs, check_vma=False)
```

```python
import functools

import jax
import jax.numpy as jnp
from jax import lax
from jax.experimental import pallas as pl
from jax.experimental.pallas import tpu as pltpu
from jax.sharding import PartitionSpec as P

adapter_scale = 2.0
lanes = 128
mebibyte = 1 << 20
over_last = (((1,), (1,)), ((), ()))
over_first = (((0,), (0,)), ((), ()))


def slot_positions(route, expert_total):
    expert_ids = lax.broadcasted_iota(jnp.int32, (1, 1, expert_total), 2)
    expert_hits = jnp.sum((route[:, :, None] == expert_ids).astype(jnp.int32), axis=1)
    earlier = jnp.cumsum(expert_hits, axis=0) - expert_hits
    return jnp.take_along_axis(earlier, route, axis=1)


def dispatched(
    output_cotangent,
    route,
    routing_weights,
    hidden,
    down_weight,
    first_adapter_factors,
    second_adapter_factors,
):
    resident, pair_one, sources, capacity, hidden_width = hidden.shape
    expert_count = lax.axis_size("expert")
    expert_total = resident * expert_count
    model_width = output_cotangent.shape[1]
    position = slot_positions(route, expert_total)
    target = route * capacity + position
    slot_cells = lax.broadcasted_iota(jnp.int32, (expert_total * capacity, 1, 1), 0)
    matches = slot_cells == target[None, :, :]
    picker = jnp.any(matches, axis=2).astype(jnp.bfloat16)
    send_rows = jnp.dot(picker, output_cotangent, preferred_element_type=jnp.float32).astype(
        jnp.bfloat16
    )
    send_rows = send_rows.reshape(expert_total, capacity, model_width)
    send_weight = jnp.sum(
        jnp.where(matches, routing_weights[None, :, :].astype(jnp.float32), 0.0), axis=(1, 2)
    )
    send_weight = send_weight.astype(jnp.bfloat16).reshape(expert_total, capacity)
    recv_rows, recv_weight = (
        lax.all_to_all(send_rows, "expert", split_axis=0, concat_axis=0, tiled=True),
        lax.all_to_all(send_weight, "expert", split_axis=0, concat_axis=0, tiled=True),
    )
    grad_rows = recv_rows.reshape(sources, resident, capacity, model_width)
    scales = recv_weight.reshape(sources, resident, capacity)
    hidden_inputs = hidden.reshape(resident, sources, capacity, hidden_width)
    reduced_rank_product = jnp.einsum(
        "bwlv,bvs->bwls", hidden_inputs, first_adapter_factors, preferred_element_type=jnp.float32
    ).astype(jnp.bfloat16)
    adapter_result = jnp.einsum(
        "nvli,nit->vnlt",
        reduced_rank_product,
        second_adapter_factors,
        preferred_element_type=jnp.float32,
    )
    fixed_output = jnp.einsum(
        "ejcf,efd->jecd",
        hidden_inputs,
        lax.all_gather(down_weight, "dp", axis=1, tiled=True),
        preferred_element_type=jnp.float32,
    )
    output_values = fixed_output + adapter_scale * adapter_result
    slot_grad = jnp.sum(grad_rows.astype(jnp.float32) * output_values, axis=3)
    scaled_result = (scales[..., None].astype(jnp.float32) * grad_rows.astype(jnp.float32)).astype(
        jnp.bfloat16
    )
    projected_down = jnp.einsum(
        "mzxl,zil->mzxi", scaled_result, second_adapter_factors, preferred_element_type=jnp.float32
    ).astype(jnp.bfloat16)
    fixed_backward = jnp.einsum(
        "jecd,efd->ejcf",
        scaled_result,
        lax.all_gather(down_weight, "dp", axis=1, tiled=True),
        preferred_element_type=jnp.float32,
    )
    activation_cotangent = fixed_backward + adapter_scale * jnp.einsum(
        "mwsa,wqa->wmsq", projected_down, first_adapter_factors, preferred_element_type=jnp.float32
    )
    hidden_cotangent = activation_cotangent.astype(jnp.bfloat16).reshape(hidden.shape)
    first_share = adapter_scale * jnp.einsum(
        "ejcf,jecr->efr", hidden_inputs, projected_down, preferred_element_type=jnp.float32
    )
    second_share = adapter_scale * jnp.einsum(
        "ejcr,jecd->erd", reduced_rank_product, scaled_result, preferred_element_type=jnp.float32
    )
    first_factor_gradient, second_factor_gradient = lax.psum((first_share, second_share), "dp")
    returned_grads = lax.all_to_all(slot_grad, "expert", split_axis=0, concat_axis=0, tiled=True)
    returned_flat = returned_grads.reshape(expert_total * capacity)
    routing_weight_gradient = jnp.sum(jnp.where(matches, returned_flat[:, None, None], 0.0), axis=0)
    return (
        hidden_cotangent,
        first_factor_gradient,
        second_factor_gradient,
        routing_weight_gradient,
    )


def start_copies(pairs, sems):
    copies = [pltpu.make_async_copy(a, b, sems.at[i]) for i, (a, b) in enumerate(pairs)]
    for copy in copies:
        copy.start()
    return copies


def pack_kernel(
    cotangent_hbm, route_hbm, weight_hbm, payload_ref, wanted_ref, route_vmem, weight_vmem, sems
):
    tokens, width = cotangent_hbm.shape
    copies = start_copies(
        [
            (route_hbm, route_vmem),
            (weight_hbm, weight_vmem),
            (cotangent_hbm, payload_ref.at[:, pl.ds(0, width)]),
        ],
        sems,
    )
    payload_ref[:, width:] = jnp.full((tokens, lanes), -1.0, jnp.bfloat16)
    copies[0].wait()
    copies[1].wait()
    wanted_ref[...] = jnp.bitwise_xor(route_vmem[...], lax.axis_index("expert"))
    both = jnp.concatenate(
        [route_vmem[...].astype(jnp.float32), weight_vmem[...].astype(jnp.float32)], axis=0
    )
    payload_ref[:16, width : width + tokens] = both.astype(jnp.bfloat16)
    copies[2].wait()


def pieces(total, size):
    return [slice(start, start + size) for start in range(0, total, size)]


def load_kernel(hidden_hbm, down_hbm, first_hbm, second_hbm, *refs):
    (hidden, down, first, second), sems = refs[:4], refs[4]
    slots = hidden.shape[0] // 2
    half = lax.axis_index("expert") // (lax.axis_size("expert") // 2)
    pairs = [(down_hbm, down), (first_hbm, first), (second_hbm, second)]
    for part in (0, 1):
        base = pl.multiple_of(jnp.bitwise_xor(half, part) * slots, slots)
        pairs.append((hidden_hbm.at[pl.ds(base, slots), :], hidden.at[pl.ds(slots * part, slots), :]))
    for copy in start_copies(pairs, sems):
        copy.wait()


def forward_kernel(
    hidden, down, first, second, low_one, low_two, out_one, out_two
):
    slots = out_one.shape[0]
    low = lax.dot_general(
        hidden[...], first[...], over_last, preferred_element_type=jnp.float32
    ).astype(jnp.bfloat16)
    low_one[...] = low[:slots]
    low_two[...] = low[slots:]
    for cut in pieces(out_one.shape[1], 512):
        values = jnp.dot(
            hidden[...], down[:, cut], preferred_element_type=jnp.float32
        ) + adapter_scale * jnp.dot(low, second[:, cut], preferred_element_type=jnp.float32)
        out_one[:, cut] = values[:slots]
        out_two[:, cut] = values[slots:]


def combine(me, capacity, blocks, out_ref, scaled_ref, pair_ref, base):
    count, tokens, width = len(blocks), blocks[0].shape[0], out_ref.shape[1]
    slots = count * capacity
    hits, weights = [], []
    for block in blocks:
        meta = block[0:16, width : width + lanes].astype(jnp.float32)
        match = meta[0:8] == me.astype(jnp.float32)
        hits.append(jnp.sum(jnp.where(match, 1.0, 0.0), axis=0, keepdims=True))
        weights.append(jnp.sum(jnp.where(match, meta[8:16], 0.0), axis=0, keepdims=True))
    hit = jnp.concatenate(hits, axis=0)
    weight = jnp.concatenate(weights, axis=0)
    before = (
        lax.broadcasted_iota(jnp.int32, (lanes, lanes), 0)
        < lax.broadcasted_iota(jnp.int32, (lanes, lanes), 1)
    )
    earlier = jnp.dot(
        hit.astype(jnp.bfloat16),
        jnp.where(before, 1.0, 0.0).astype(jnp.bfloat16),
        preferred_element_type=jnp.float32,
    )
    source = jnp.bitwise_xor(lax.broadcasted_iota(jnp.int32, (count, lanes), 0), me % count)
    target = jnp.where(hit > 0.0, (source * capacity).astype(jnp.float32) + earlier, -1.0)
    per = lanes // tokens
    lane = lax.broadcasted_iota(jnp.int32, (1, lanes), 1)
    slot = lax.broadcasted_iota(jnp.int32, (slots, lanes), 0).astype(jnp.float32)

    def merged(rows, q):
        row = rows[per * q : per * q + 1]
        for r in range(1, per):
            shifted = pltpu.roll(rows[per * q + r : per * q + r + 1], tokens * r, 1)
            row = jnp.where(lane >= tokens * r, shifted, row)
        return row

    picks, column = [], jnp.zeros((slots, 1), jnp.float32)
    for q in range(count // per):
        pick = jnp.where(slot == merged(target, q), 1.0, 0.0)
        column = column + jnp.sum(pick * merged(weight, q), axis=1, keepdims=True)
        picks.append(pick)
    picker = jnp.concatenate([pick.astype(jnp.bfloat16) for pick in picks], axis=1)
    grads = jnp.zeros((slots, 1), jnp.float32)
    for cut in pieces(width, 512):
        gathered_rows = jnp.concatenate([block[:, cut] for block in blocks], axis=0)
        rows = jnp.dot(picker, gathered_rows, preferred_element_type=jnp.float32)
        grads = grads + jnp.sum(rows * out_ref[:, cut], axis=1, keepdims=True)
        scaled_ref[:, cut] = (rows * column).astype(jnp.bfloat16)
    for q in range(count // per):
        row = jnp.sum(picks[q] * grads, axis=0, keepdims=True)
        for r in range(per):
            s = base + per * q + r
            pair_ref[s : s + 1, :] = row if r == 0 else pltpu.roll(row, lanes - tokens * r, 1)


def factor_sums(part, scaled_ref, low_ref, hidden_ref, second_ref):
    slots = scaled_ref.shape[0]
    scaled = scaled_ref[...]
    lowered = lax.dot_general(
        scaled, second_ref[...], over_last, preferred_element_type=jnp.float32
    ).astype(jnp.bfloat16)
    hidden = hidden_ref[slots * part : slots * (part + 1), :]
    first = lax.dot_general(lowered, hidden, over_first, preferred_element_type=jnp.float32)
    second = lax.dot_general(
        low_ref[...], scaled, over_first, preferred_element_type=jnp.float32
    )
    return lowered, adapter_scale * first, adapter_scale * second


def first_kernel(count, capacity, *refs):
    blocks, refs = refs[:count], refs[count:]
    out_ref, low_ref, hidden_ref, second_ref = refs[:4]
    scaled_ref, lowered_ref, dfirst_ref, dsecond_ref, pair_ref = refs[4:]
    combine(lax.axis_index("expert"), capacity, blocks, out_ref, scaled_ref, pair_ref, 0)
    lowered_ref[...], dfirst_ref[...], dsecond_ref[...] = factor_sums(
        0, scaled_ref, low_ref, hidden_ref, second_ref
    )


def combine_kernel(count, capacity, *refs):
    blocks, (out_ref, before_ref, scaled_ref, pair_ref) = refs[:count], refs[count:]
    pair_ref[:count, :] = before_ref[...]
    combine(
        lax.axis_index("expert"), capacity, blocks, out_ref, scaled_ref, pair_ref, count
    )


def cotangent_of(scaled_ref, lowered, down_ref, first_ref):
    fixed = lax.dot_general(
        scaled_ref[...], down_ref[...], over_last, preferred_element_type=jnp.float32
    )
    adapter = jnp.dot(lowered, first_ref[...], preferred_element_type=jnp.float32)
    return (fixed + adapter_scale * adapter).astype(jnp.bfloat16)


def late_kernel(
    scaled_ref,
    low_ref,
    hidden_ref,
    down_ref,
    first_ref,
    second_ref,
    dfirst_before,
    dsecond_before,
    cot_ref,
    dfirst_ref,
    dsecond_ref,
):
    lowered, dfirst, dsecond = factor_sums(1, scaled_ref, low_ref, hidden_ref, second_ref)
    dfirst_ref[...] = dfirst + dfirst_before[...]
    dsecond_ref[...] = dsecond + dsecond_before[...]
    cot_ref[...] = cotangent_of(scaled_ref, lowered, down_ref, first_ref)


def cotangent_kernel(count, scaled_ref, lowered_ref, down_ref, first_ref, late_ref, cot_ref):
    half = lax.axis_index("expert") // count
    slots = scaled_ref.shape[0]
    here = pl.ds(pl.multiple_of(half * slots, slots), slots)
    there = pl.ds(pl.multiple_of((1 - half) * slots, slots), slots)
    cot_ref[there, :] = late_ref[...]
    cot_ref[here, :] = cotangent_of(scaled_ref, lowered_ref[...], down_ref, first_ref)


def gathered(
    output_cotangent,
    route,
    routing_weights,
    hidden,
    down_weight,
    first_adapter_factors,
    second_adapter_factors,
):
    _, _, sources, capacity, hidden_width = hidden.shape
    tokens, width = output_cotangent.shape
    rank = first_adapter_factors.shape[2]
    count = lax.axis_size("expert")
    slots = sources * capacity
    half = count // 2
    bf16, f32 = jnp.bfloat16, jnp.float32

    def swap(array, distance):
        return lax.ppermute(array, "expert", [(i, i ^ distance) for i in range(count)])

    def call(limit, kernel, outs, spaces, scratch, *operands, plain=()):
        return pl.pallas_call(
            kernel,
            out_shape=tuple(
                jax.ShapeDtypeStruct(*out) if i in plain else pltpu.VMEM(*out)
                for i, out in enumerate(outs)
            ),
            in_specs=[pl.BlockSpec(memory_space=space) for space in spaces],
            out_specs=(pl.BlockSpec(memory_space=pltpu.VMEM),) * len(outs),
            scratch_shapes=scratch,
            compiler_params=pltpu.CompilerParams(vmem_limit_bytes=limit * mebibyte),
            name=getattr(kernel, "func", kernel).__name__,
        )(*map(pltpu.with_memory_space_constraint, operands, spaces))

    route_rows = route.T
    payload, wanted = call(
        8,
        pack_kernel,
        [((tokens, width + lanes), bf16), (route_rows.shape, jnp.int32)],
        [pltpu.HBM] * 3,
        [
            pltpu.VMEM(route_rows.shape, jnp.int32),
            pltpu.VMEM(route_rows.shape, bf16),
            pltpu.SemaphoreType.DMA((3,)),
        ],
        output_cotangent,
        route_rows,
        routing_weights.T,
    )
    blocks = {0: payload}
    far = [d for d in range(4, count, 4)]
    near = [d for d in far if d < half]
    late = [d for d in far if d >= half]
    direct = [d for d in far if d & (d - 1) == 0]
    for d in direct[::-1]:
        blocks[d] = swap(payload, d)
    blocks[2] = swap(payload, 2)
    parameters = (
        hidden.reshape(slots, hidden_width),
        down_weight[0],
        first_adapter_factors[0].T,
        second_adapter_factors[0],
    )
    held = call(
        8,
        load_kernel,
        [(array.shape, bf16) for array in parameters],
        [pltpu.HBM] * 4,
        [pltpu.SemaphoreType.DMA((5,))],
        *parameters,
    )
    blocks[near[0]], held = lax.optimization_barrier((blocks[near[0]], held))
    low, low_late, out, out_late = call(
        24,
        forward_kernel,
        [((slots // 2, rank), bf16)] * 2 + [((slots // 2, width), f32)] * 2,
        [pltpu.VMEM] * 4,
        [],
        *held,
    )

    for d in far:
        if d not in direct:
            blocks[d] = swap(blocks[half], d - half)
    for d in far:
        blocks[d + 2] = swap(blocks[d], 2)
    for d in [0] + near:
        blocks[d + 1] = swap(blocks[d], 1)
        blocks[d + 3] = swap(blocks[d + 2], 1)
    hidden_held, down, first, second = held
    grads = [((rank, hidden_width), f32), ((rank, width), f32)]
    lowered = ((slots // 2, rank), bf16)
    scaled, *partial, pair = call(
        24,
        functools.partial(first_kernel, half, capacity),
        [((slots // 2, width), bf16), lowered, *grads, ((half, lanes), f32)],
        [pltpu.VMEM] * (half + 4),
        [],
        *[blocks[s] for s in range(half)],
        out,
        low,
        hidden_held,
        second,
    )
    for d in late:
        blocks[d + 2], partial, pair = lax.optimization_barrier((blocks[d + 2], partial, pair))
        blocks[d + 1] = swap(blocks[d], 1)
        blocks[d + 3] = swap(blocks[d + 2], 1)
    lowered_early, dfirst, dsecond = partial
    scaled_late, pair = call(
        24,
        functools.partial(combine_kernel, half, capacity),
        [((slots // 2, width), bf16), ((count, lanes), f32)],
        [pltpu.VMEM] * (half + 2),
        [],
        *[blocks[s] for s in range(half, count)],
        out_late,
        pair,
    )
    late_rows = ((slots // 2, hidden_width), bf16)
    cotangent, dfirst, dsecond = call(
        24,
        late_kernel,
        [late_rows, *grads],
        [pltpu.VMEM] * 8,
        [],
        scaled_late,
        low_late,
        *held,
        dfirst,
        dsecond,
        plain=(1, 2),
    )

    distance = lax.broadcasted_iota(jnp.int32, pair.shape, 0)
    order = near + late[::-1]
    moved = [swap(pair, d) for d in order]
    for d, values in zip(order, moved):
        pair = jnp.where(distance - jnp.bitwise_and(distance, 3) == d, values, pair)
    pair, cotangent, dfirst, dsecond = lax.optimization_barrier(
        (pair, cotangent, dfirst, dsecond)
    )
    (cotangent,) = call(
        24,
        functools.partial(cotangent_kernel, half),
        [((slots, hidden_width), bf16)],
        [pltpu.VMEM] * 5,
        [],
        scaled,
        lowered_early,
        down,
        first,
        cotangent,
        plain=(0,),
    )
    moved = [swap(pair, d) for d in (1, 2, 3)]
    for d, values in zip((1, 2, 3), moved):
        pair = jnp.where(jnp.bitwise_and(distance, 3) == d, values, pair)
    hop = lax.broadcasted_iota(jnp.int32, (count, 1, 1), 0)
    gradient = jnp.sum(jnp.where(wanted[None] == hop, pair[:, None, :tokens], 0.0), axis=0)
    return (
        cotangent.reshape(hidden.shape),
        dfirst.T[None],
        dsecond[None],
        gradient.T,
    )


def local(output_cotangent, route, routing_weights, hidden, *parameters):
    resident, pairs, sources, capacity, hidden_width = hidden.shape
    count = lax.axis_size("expert")
    tokens, top = route.shape
    gather = (
        pairs * lax.axis_size("dp") == 1
        and resident == 1
        and sources == count
        and count & (count - 1) == 0
        and 16 <= count <= 256
        and lanes % tokens == 0
        and (count // 2) % (lanes // tokens) == 0
        and (count // 2 * capacity) % 16 == 0
        and output_cotangent.shape[1] % 512 == 0
        and hidden_width % 256 == 0
        and top == 8
        and 16 <= tokens <= 2 * capacity
    )
    form = gathered if gather else dispatched
    return form(output_cotangent, route, routing_weights, hidden, *parameters)


def solution(mesh):
    in_specs = (
        P(("groups", "expert", "dp"), None),
        P(("groups", "expert", "dp"), None),
        P(("groups", "expert", "dp"), None),
        P(("groups", "expert"), "dp", None, None, None),
        P("expert", "dp", None),
        P("expert", None, None),
        P("expert", None, None),
    )
    out_specs = (
        P(("groups", "expert"), "dp", None, None, None),
        P(("groups", "expert"), None, None),
        P(("groups", "expert"), None, None),
        P(("groups", "expert", "dp"), None),
    )
    return jax.shard_map(local, mesh=mesh, in_specs=in_specs, out_specs=out_specs, check_vma=False)
```

```python
import functools

import jax
import jax.numpy as jnp
from jax import lax
from jax.experimental import pallas as pl
from jax.experimental.pallas import tpu as pltpu
from jax.sharding import PartitionSpec as P

adapter_scale = 2.0
lanes = 128
mebibyte = 1 << 20
over_last = (((1,), (1,)), ((), ()))
over_first = (((0,), (0,)), ((), ()))


def slot_positions(route, expert_total):
    expert_ids = lax.broadcasted_iota(jnp.int32, (1, 1, expert_total), 2)
    expert_hits = jnp.sum((route[:, :, None] == expert_ids).astype(jnp.int32), axis=1)
    earlier = jnp.cumsum(expert_hits, axis=0) - expert_hits
    return jnp.take_along_axis(earlier, route, axis=1)


def dispatched(
    output_cotangent,
    route,
    routing_weights,
    hidden,
    down_weight,
    first_adapter_factors,
    second_adapter_factors,
):
    resident, pair_one, sources, capacity, hidden_width = hidden.shape
    expert_count = lax.axis_size("expert")
    expert_total = resident * expert_count
    model_width = output_cotangent.shape[1]
    position = slot_positions(route, expert_total)
    target = route * capacity + position
    slot_cells = lax.broadcasted_iota(jnp.int32, (expert_total * capacity, 1, 1), 0)
    matches = slot_cells == target[None, :, :]
    picker = jnp.any(matches, axis=2).astype(jnp.bfloat16)
    send_rows = jnp.dot(picker, output_cotangent, preferred_element_type=jnp.float32).astype(
        jnp.bfloat16
    )
    send_rows = send_rows.reshape(expert_total, capacity, model_width)
    send_weight = jnp.sum(
        jnp.where(matches, routing_weights[None, :, :].astype(jnp.float32), 0.0), axis=(1, 2)
    )
    send_weight = send_weight.astype(jnp.bfloat16).reshape(expert_total, capacity)
    recv_rows, recv_weight = (
        lax.all_to_all(send_rows, "expert", split_axis=0, concat_axis=0, tiled=True),
        lax.all_to_all(send_weight, "expert", split_axis=0, concat_axis=0, tiled=True),
    )
    grad_rows = recv_rows.reshape(sources, resident, capacity, model_width)
    scales = recv_weight.reshape(sources, resident, capacity)
    hidden_inputs = hidden.reshape(resident, sources, capacity, hidden_width)
    reduced_rank_product = jnp.einsum(
        "bwlv,bvs->bwls", hidden_inputs, first_adapter_factors, preferred_element_type=jnp.float32
    ).astype(jnp.bfloat16)
    adapter_result = jnp.einsum(
        "nvli,nit->vnlt",
        reduced_rank_product,
        second_adapter_factors,
        preferred_element_type=jnp.float32,
    )
    fixed_output = jnp.einsum(
        "ejcf,efd->jecd",
        hidden_inputs,
        lax.all_gather(down_weight, "dp", axis=1, tiled=True),
        preferred_element_type=jnp.float32,
    )
    output_values = fixed_output + adapter_scale * adapter_result
    slot_grad = jnp.sum(grad_rows.astype(jnp.float32) * output_values, axis=3)
    scaled_result = (scales[..., None].astype(jnp.float32) * grad_rows.astype(jnp.float32)).astype(
        jnp.bfloat16
    )
    projected_down = jnp.einsum(
        "mzxl,zil->mzxi", scaled_result, second_adapter_factors, preferred_element_type=jnp.float32
    ).astype(jnp.bfloat16)
    fixed_backward = jnp.einsum(
        "jecd,efd->ejcf",
        scaled_result,
        lax.all_gather(down_weight, "dp", axis=1, tiled=True),
        preferred_element_type=jnp.float32,
    )
    activation_cotangent = fixed_backward + adapter_scale * jnp.einsum(
        "mwsa,wqa->wmsq", projected_down, first_adapter_factors, preferred_element_type=jnp.float32
    )
    hidden_cotangent = activation_cotangent.astype(jnp.bfloat16).reshape(hidden.shape)
    first_share = adapter_scale * jnp.einsum(
        "ejcf,jecr->efr", hidden_inputs, projected_down, preferred_element_type=jnp.float32
    )
    second_share = adapter_scale * jnp.einsum(
        "ejcr,jecd->erd", reduced_rank_product, scaled_result, preferred_element_type=jnp.float32
    )
    first_factor_gradient, second_factor_gradient = lax.psum((first_share, second_share), "dp")
    returned_grads = lax.all_to_all(slot_grad, "expert", split_axis=0, concat_axis=0, tiled=True)
    returned_flat = returned_grads.reshape(expert_total * capacity)
    routing_weight_gradient = jnp.sum(jnp.where(matches, returned_flat[:, None, None], 0.0), axis=0)
    return (
        hidden_cotangent,
        first_factor_gradient,
        second_factor_gradient,
        routing_weight_gradient,
    )


def start_copies(pairs, sems):
    copies = [pltpu.make_async_copy(a, b, sems.at[i]) for i, (a, b) in enumerate(pairs)]
    for copy in copies:
        copy.start()
    return copies


def pack_kernel(
    cotangent_hbm, route_hbm, weight_hbm, payload_ref, wanted_ref, route_vmem, weight_vmem, sems
):
    tokens, width = cotangent_hbm.shape
    copies = start_copies(
        [
            (route_hbm, route_vmem),
            (weight_hbm, weight_vmem),
            (cotangent_hbm, payload_ref.at[:, pl.ds(0, width)]),
        ],
        sems,
    )
    payload_ref[:, width:] = jnp.full((tokens, lanes), -1.0, jnp.bfloat16)
    copies[0].wait()
    copies[1].wait()
    wanted_ref[...] = jnp.bitwise_xor(route_vmem[...], lax.axis_index("expert"))
    both = jnp.concatenate(
        [route_vmem[...].astype(jnp.float32), weight_vmem[...].astype(jnp.float32)], axis=0
    )
    payload_ref[:16, width : width + tokens] = both.astype(jnp.bfloat16)
    copies[2].wait()


def pieces(total, size):
    return [slice(start, start + size) for start in range(0, total, size)]


def load_kernel(hidden_hbm, down_hbm, first_hbm, second_hbm, *refs):
    (hidden, down, first, second), sems = refs[:4], refs[4]
    slots = hidden.shape[0] // 2
    half = lax.axis_index("expert") // (lax.axis_size("expert") // 2)
    pairs = [(down_hbm, down), (first_hbm, first), (second_hbm, second)]
    for part in (0, 1):
        base = pl.multiple_of(jnp.bitwise_xor(half, part) * slots, slots)
        pairs.append((hidden_hbm.at[pl.ds(base, slots), :], hidden.at[pl.ds(slots * part, slots), :]))
    for copy in start_copies(pairs, sems):
        copy.wait()


def forward_kernel(
    hidden, down, first, second, low_one, low_two, out_one, out_two
):
    slots = out_one.shape[0]
    low = lax.dot_general(
        hidden[...], first[...], over_last, preferred_element_type=jnp.float32
    ).astype(jnp.bfloat16)
    low_one[...] = low[:slots]
    low_two[...] = low[slots:]
    for cut in pieces(out_one.shape[1], 512):
        values = jnp.dot(
            hidden[...], down[:, cut], preferred_element_type=jnp.float32
        ) + adapter_scale * jnp.dot(low, second[:, cut], preferred_element_type=jnp.float32)
        out_one[:, cut] = values[:slots]
        out_two[:, cut] = values[slots:]


def combine(me, capacity, blocks, out_ref, scaled_ref, pair_ref, base):
    count, tokens, width = len(blocks), blocks[0].shape[0], out_ref.shape[1]
    slots = count * capacity
    hits, weights = [], []
    for block in blocks:
        meta = block[0:16, width : width + lanes].astype(jnp.float32)
        match = meta[0:8] == me.astype(jnp.float32)
        hits.append(jnp.sum(jnp.where(match, 1.0, 0.0), axis=0, keepdims=True))
        weights.append(jnp.sum(jnp.where(match, meta[8:16], 0.0), axis=0, keepdims=True))
    hit = jnp.concatenate(hits, axis=0)
    weight = jnp.concatenate(weights, axis=0)
    before = (
        lax.broadcasted_iota(jnp.int32, (lanes, lanes), 0)
        < lax.broadcasted_iota(jnp.int32, (lanes, lanes), 1)
    )
    earlier = jnp.dot(
        hit.astype(jnp.bfloat16),
        jnp.where(before, 1.0, 0.0).astype(jnp.bfloat16),
        preferred_element_type=jnp.float32,
    )
    source = jnp.bitwise_xor(lax.broadcasted_iota(jnp.int32, (count, lanes), 0), me % count)
    target = jnp.where(hit > 0.0, (source * capacity).astype(jnp.float32) + earlier, -1.0)
    per = lanes // tokens
    lane = lax.broadcasted_iota(jnp.int32, (1, lanes), 1)
    slot = lax.broadcasted_iota(jnp.int32, (slots, lanes), 0).astype(jnp.float32)

    def merged(rows, q):
        row = rows[per * q : per * q + 1]
        for r in range(1, per):
            shifted = pltpu.roll(rows[per * q + r : per * q + r + 1], tokens * r, 1)
            row = jnp.where(lane >= tokens * r, shifted, row)
        return row

    picks, column = [], jnp.zeros((slots, 1), jnp.float32)
    for q in range(count // per):
        pick = jnp.where(slot == merged(target, q), 1.0, 0.0)
        column = column + jnp.sum(pick * merged(weight, q), axis=1, keepdims=True)
        picks.append(pick)
    picker = jnp.concatenate([pick.astype(jnp.bfloat16) for pick in picks], axis=1)
    grads = jnp.zeros((slots, 1), jnp.float32)
    for cut in pieces(width, 512):
        gathered_rows = jnp.concatenate([block[:, cut] for block in blocks], axis=0)
        rows = jnp.dot(picker, gathered_rows, preferred_element_type=jnp.float32)
        grads = grads + jnp.sum(rows * out_ref[:, cut], axis=1, keepdims=True)
        scaled_ref[:, cut] = (rows * column).astype(jnp.bfloat16)
    for q in range(count // per):
        row = jnp.sum(picks[q] * grads, axis=0, keepdims=True)
        for r in range(per):
            s = base + per * q + r
            pair_ref[s : s + 1, :] = row if r == 0 else pltpu.roll(row, lanes - tokens * r, 1)


def factor_sums(part, scaled_ref, low_ref, hidden_ref, second_ref):
    slots = scaled_ref.shape[0]
    scaled = scaled_ref[...]
    lowered = lax.dot_general(
        scaled, second_ref[...], over_last, preferred_element_type=jnp.float32
    ).astype(jnp.bfloat16)
    hidden = hidden_ref[slots * part : slots * (part + 1), :]
    first = lax.dot_general(lowered, hidden, over_first, preferred_element_type=jnp.float32)
    second = lax.dot_general(
        low_ref[...], scaled, over_first, preferred_element_type=jnp.float32
    )
    return lowered, adapter_scale * first, adapter_scale * second


def first_kernel(count, capacity, *refs):
    blocks, refs = refs[:count], refs[count:]
    out_ref, low_ref, hidden_ref, second_ref = refs[:4]
    scaled_ref, lowered_ref, dfirst_ref, dsecond_ref, pair_ref = refs[4:]
    combine(lax.axis_index("expert"), capacity, blocks, out_ref, scaled_ref, pair_ref, 0)
    lowered_ref[...], dfirst_ref[...], dsecond_ref[...] = factor_sums(
        0, scaled_ref, low_ref, hidden_ref, second_ref
    )


def combine_kernel(count, capacity, *refs):
    blocks, (out_ref, before_ref, scaled_ref, pair_ref) = refs[:count], refs[count:]
    pair_ref[:count, :] = before_ref[...]
    combine(
        lax.axis_index("expert"), capacity, blocks, out_ref, scaled_ref, pair_ref, count
    )


def cotangent_of(scaled_ref, lowered, down_ref, first_ref):
    fixed = lax.dot_general(
        scaled_ref[...], down_ref[...], over_last, preferred_element_type=jnp.float32
    )
    adapter = jnp.dot(lowered, first_ref[...], preferred_element_type=jnp.float32)
    return (fixed + adapter_scale * adapter).astype(jnp.bfloat16)


def late_kernel(
    scaled_ref,
    low_ref,
    hidden_ref,
    down_ref,
    first_ref,
    second_ref,
    dfirst_before,
    dsecond_before,
    cot_ref,
    dfirst_ref,
    dsecond_ref,
):
    lowered, dfirst, dsecond = factor_sums(1, scaled_ref, low_ref, hidden_ref, second_ref)
    dfirst_ref[...] = dfirst + dfirst_before[...]
    dsecond_ref[...] = dsecond + dsecond_before[...]
    cot_ref[...] = cotangent_of(scaled_ref, lowered, down_ref, first_ref)


def cotangent_kernel(count, scaled_ref, lowered_ref, down_ref, first_ref, late_ref, cot_ref):
    half = lax.axis_index("expert") // count
    slots = scaled_ref.shape[0]
    here = pl.ds(pl.multiple_of(half * slots, slots), slots)
    there = pl.ds(pl.multiple_of((1 - half) * slots, slots), slots)
    cot_ref[there, :] = late_ref[...]
    cot_ref[here, :] = cotangent_of(scaled_ref, lowered_ref[...], down_ref, first_ref)


def gathered(
    output_cotangent,
    route,
    routing_weights,
    hidden,
    down_weight,
    first_adapter_factors,
    second_adapter_factors,
):
    _, _, sources, capacity, hidden_width = hidden.shape
    tokens, width = output_cotangent.shape
    rank = first_adapter_factors.shape[2]
    count = lax.axis_size("expert")
    slots = sources * capacity
    half = count // 2
    bf16, f32 = jnp.bfloat16, jnp.float32

    def swap(array, distance):
        return lax.ppermute(array, "expert", [(i, i ^ distance) for i in range(count)])

    def call(limit, kernel, outs, spaces, scratch, *operands, plain=()):
        return pl.pallas_call(
            kernel,
            out_shape=tuple(
                jax.ShapeDtypeStruct(*out) if i in plain else pltpu.VMEM(*out)
                for i, out in enumerate(outs)
            ),
            in_specs=[pl.BlockSpec(memory_space=space) for space in spaces],
            out_specs=(pl.BlockSpec(memory_space=pltpu.VMEM),) * len(outs),
            scratch_shapes=scratch,
            compiler_params=pltpu.CompilerParams(vmem_limit_bytes=limit * mebibyte),
            name=getattr(kernel, "func", kernel).__name__,
        )(*map(pltpu.with_memory_space_constraint, operands, spaces))

    route_rows = route.T
    payload, wanted = call(
        8,
        pack_kernel,
        [((tokens, width + lanes), bf16), (route_rows.shape, jnp.int32)],
        [pltpu.HBM] * 3,
        [
            pltpu.VMEM(route_rows.shape, jnp.int32),
            pltpu.VMEM(route_rows.shape, bf16),
            pltpu.SemaphoreType.DMA((3,)),
        ],
        output_cotangent,
        route_rows,
        routing_weights.T,
    )
    blocks = {0: payload}
    far = [d for d in range(4, count, 4)]
    near = [d for d in far if d < half]
    late = [d for d in far if d >= half]
    direct = [d for d in far if d & (d - 1) == 0]
    for d in direct[::-1]:
        blocks[d] = swap(payload, d)
    blocks[2] = swap(payload, 2)
    parameters = (
        hidden.reshape(slots, hidden_width),
        down_weight[0],
        first_adapter_factors[0].T,
        second_adapter_factors[0],
    )
    held = call(
        8,
        load_kernel,
        [(array.shape, bf16) for array in parameters],
        [pltpu.HBM] * 4,
        [pltpu.SemaphoreType.DMA((5,))],
        *parameters,
    )
    blocks[near[0]], held = lax.optimization_barrier((blocks[near[0]], held))
    low, low_late, out, out_late = call(
        24,
        forward_kernel,
        [((slots // 2, rank), bf16)] * 2 + [((slots // 2, width), f32)] * 2,
        [pltpu.VMEM] * 4,
        [],
        *held,
    )

    for d in far:
        if d not in direct:
            blocks[d] = swap(blocks[half], d - half)
    for d in far:
        blocks[d + 2] = swap(blocks[d], 2)
    for d in [0] + near:
        blocks[d + 1] = swap(blocks[d], 1)
        blocks[d + 3] = swap(blocks[d + 2], 1)
    hidden_held, down, first, second = held
    grads = [((rank, hidden_width), f32), ((rank, width), f32)]
    lowered = ((slots // 2, rank), bf16)
    scaled, *partial, pair = call(
        24,
        functools.partial(first_kernel, half, capacity),
        [((slots // 2, width), bf16), lowered, *grads, ((half, lanes), f32)],
        [pltpu.VMEM] * (half + 4),
        [],
        *[blocks[s] for s in range(half)],
        out,
        low,
        hidden_held,
        second,
    )
    d = late[-1] + 2
    blocks[d], partial, pair = lax.optimization_barrier((blocks[d], partial, pair))
    for d in late:
        blocks[d + 1] = swap(blocks[d], 1)
        blocks[d + 3] = swap(blocks[d + 2], 1)
    lowered_early, dfirst, dsecond = partial
    scaled_late, pair = call(
        24,
        functools.partial(combine_kernel, half, capacity),
        [((slots // 2, width), bf16), ((count, lanes), f32)],
        [pltpu.VMEM] * (half + 2),
        [],
        *[blocks[s] for s in range(half, count)],
        out_late,
        pair,
    )
    late_rows = ((slots // 2, hidden_width), bf16)
    cotangent, dfirst, dsecond = call(
        24,
        late_kernel,
        [late_rows, *grads],
        [pltpu.VMEM] * 8,
        [],
        scaled_late,
        low_late,
        *held,
        dfirst,
        dsecond,
        plain=(1, 2),
    )

    distance = lax.broadcasted_iota(jnp.int32, pair.shape, 0)
    order = near + late[::-1]
    moved = [swap(pair, d) for d in order]
    for d, values in zip(order, moved):
        pair = jnp.where(distance - jnp.bitwise_and(distance, 3) == d, values, pair)
    pair, cotangent, dfirst, dsecond = lax.optimization_barrier(
        (pair, cotangent, dfirst, dsecond)
    )
    (cotangent,) = call(
        24,
        functools.partial(cotangent_kernel, half),
        [((slots, hidden_width), bf16)],
        [pltpu.VMEM] * 5,
        [],
        scaled,
        lowered_early,
        down,
        first,
        cotangent,
        plain=(0,),
    )
    moved = [swap(pair, d) for d in (1, 2, 3)]
    for d, values in zip((1, 2, 3), moved):
        pair = jnp.where(jnp.bitwise_and(distance, 3) == d, values, pair)
    hop = lax.broadcasted_iota(jnp.int32, (count, 1, 1), 0)
    gradient = jnp.sum(jnp.where(wanted[None] == hop, pair[:, None, :tokens], 0.0), axis=0)
    return (
        cotangent.reshape(hidden.shape),
        dfirst.T[None],
        dsecond[None],
        gradient.T,
    )


def local(output_cotangent, route, routing_weights, hidden, *parameters):
    resident, pairs, sources, capacity, hidden_width = hidden.shape
    count = lax.axis_size("expert")
    tokens, top = route.shape
    gather = (
        pairs * lax.axis_size("dp") == 1
        and resident == 1
        and sources == count
        and count & (count - 1) == 0
        and 16 <= count <= 256
        and lanes % tokens == 0
        and (count // 2) % (lanes // tokens) == 0
        and (count // 2 * capacity) % 16 == 0
        and output_cotangent.shape[1] % 512 == 0
        and hidden_width % 256 == 0
        and top == 8
        and 16 <= tokens <= 2 * capacity
    )
    form = gathered if gather else dispatched
    return form(output_cotangent, route, routing_weights, hidden, *parameters)


def solution(mesh):
    in_specs = (
        P(("groups", "expert", "dp"), None),
        P(("groups", "expert", "dp"), None),
        P(("groups", "expert", "dp"), None),
        P(("groups", "expert"), "dp", None, None, None),
        P("expert", "dp", None),
        P("expert", None, None),
        P("expert", None, None),
    )
    out_specs = (
        P(("groups", "expert"), "dp", None, None, None),
        P(("groups", "expert"), None, None),
        P(("groups", "expert"), None, None),
        P(("groups", "expert", "dp"), None),
    )
    return jax.shard_map(local, mesh=mesh, in_specs=in_specs, out_specs=out_specs, check_vma=False)
```

```python
import functools

import jax
import jax.numpy as jnp
from jax import lax
from jax.experimental import pallas as pl
from jax.experimental.pallas import tpu as pltpu
from jax.sharding import PartitionSpec as P

adapter_scale = 2.0
lanes = 128
mebibyte = 1 << 20
over_last = (((1,), (1,)), ((), ()))
over_first = (((0,), (0,)), ((), ()))


def slot_positions(route, expert_total):
    expert_ids = lax.broadcasted_iota(jnp.int32, (1, 1, expert_total), 2)
    expert_hits = jnp.sum((route[:, :, None] == expert_ids).astype(jnp.int32), axis=1)
    earlier = jnp.cumsum(expert_hits, axis=0) - expert_hits
    return jnp.take_along_axis(earlier, route, axis=1)


def dispatched(
    output_cotangent,
    route,
    routing_weights,
    hidden,
    down_weight,
    first_adapter_factors,
    second_adapter_factors,
):
    resident, pair_one, sources, capacity, hidden_width = hidden.shape
    expert_count = lax.axis_size("expert")
    expert_total = resident * expert_count
    model_width = output_cotangent.shape[1]
    position = slot_positions(route, expert_total)
    target = route * capacity + position
    slot_cells = lax.broadcasted_iota(jnp.int32, (expert_total * capacity, 1, 1), 0)
    matches = slot_cells == target[None, :, :]
    picker = jnp.any(matches, axis=2).astype(jnp.bfloat16)
    send_rows = jnp.dot(picker, output_cotangent, preferred_element_type=jnp.float32).astype(
        jnp.bfloat16
    )
    send_rows = send_rows.reshape(expert_total, capacity, model_width)
    send_weight = jnp.sum(
        jnp.where(matches, routing_weights[None, :, :].astype(jnp.float32), 0.0), axis=(1, 2)
    )
    send_weight = send_weight.astype(jnp.bfloat16).reshape(expert_total, capacity)
    recv_rows, recv_weight = (
        lax.all_to_all(send_rows, "expert", split_axis=0, concat_axis=0, tiled=True),
        lax.all_to_all(send_weight, "expert", split_axis=0, concat_axis=0, tiled=True),
    )
    grad_rows = recv_rows.reshape(sources, resident, capacity, model_width)
    scales = recv_weight.reshape(sources, resident, capacity)
    hidden_inputs = hidden.reshape(resident, sources, capacity, hidden_width)
    reduced_rank_product = jnp.einsum(
        "bwlv,bvs->bwls", hidden_inputs, first_adapter_factors, preferred_element_type=jnp.float32
    ).astype(jnp.bfloat16)
    adapter_result = jnp.einsum(
        "nvli,nit->vnlt",
        reduced_rank_product,
        second_adapter_factors,
        preferred_element_type=jnp.float32,
    )
    fixed_output = jnp.einsum(
        "ejcf,efd->jecd",
        hidden_inputs,
        lax.all_gather(down_weight, "dp", axis=1, tiled=True),
        preferred_element_type=jnp.float32,
    )
    output_values = fixed_output + adapter_scale * adapter_result
    slot_grad = jnp.sum(grad_rows.astype(jnp.float32) * output_values, axis=3)
    scaled_result = (scales[..., None].astype(jnp.float32) * grad_rows.astype(jnp.float32)).astype(
        jnp.bfloat16
    )
    projected_down = jnp.einsum(
        "mzxl,zil->mzxi", scaled_result, second_adapter_factors, preferred_element_type=jnp.float32
    ).astype(jnp.bfloat16)
    fixed_backward = jnp.einsum(
        "jecd,efd->ejcf",
        scaled_result,
        lax.all_gather(down_weight, "dp", axis=1, tiled=True),
        preferred_element_type=jnp.float32,
    )
    activation_cotangent = fixed_backward + adapter_scale * jnp.einsum(
        "mwsa,wqa->wmsq", projected_down, first_adapter_factors, preferred_element_type=jnp.float32
    )
    hidden_cotangent = activation_cotangent.astype(jnp.bfloat16).reshape(hidden.shape)
    first_share = adapter_scale * jnp.einsum(
        "ejcf,jecr->efr", hidden_inputs, projected_down, preferred_element_type=jnp.float32
    )
    second_share = adapter_scale * jnp.einsum(
        "ejcr,jecd->erd", reduced_rank_product, scaled_result, preferred_element_type=jnp.float32
    )
    first_factor_gradient, second_factor_gradient = lax.psum((first_share, second_share), "dp")
    returned_grads = lax.all_to_all(slot_grad, "expert", split_axis=0, concat_axis=0, tiled=True)
    returned_flat = returned_grads.reshape(expert_total * capacity)
    routing_weight_gradient = jnp.sum(jnp.where(matches, returned_flat[:, None, None], 0.0), axis=0)
    return (
        hidden_cotangent,
        first_factor_gradient,
        second_factor_gradient,
        routing_weight_gradient,
    )


def start_copies(pairs, sems):
    copies = [pltpu.make_async_copy(a, b, sems.at[i]) for i, (a, b) in enumerate(pairs)]
    for copy in copies:
        copy.start()
    return copies


def pack_kernel(
    cotangent_hbm, route_hbm, weight_hbm, payload_ref, wanted_ref, route_vmem, weight_vmem, sems
):
    tokens, width = cotangent_hbm.shape
    copies = start_copies(
        [
            (route_hbm, route_vmem),
            (weight_hbm, weight_vmem),
            (cotangent_hbm, payload_ref.at[:, pl.ds(0, width)]),
        ],
        sems,
    )
    payload_ref[:, width:] = jnp.full((tokens, lanes), -1.0, jnp.bfloat16)
    copies[0].wait()
    copies[1].wait()
    wanted_ref[...] = jnp.bitwise_xor(route_vmem[...], lax.axis_index("expert"))
    both = jnp.concatenate(
        [route_vmem[...].astype(jnp.float32), weight_vmem[...].astype(jnp.float32)], axis=0
    )
    payload_ref[:16, width : width + tokens] = both.astype(jnp.bfloat16)
    copies[2].wait()


def pieces(total, size):
    return [slice(start, start + size) for start in range(0, total, size)]


def load_kernel(hidden_hbm, down_hbm, first_hbm, second_hbm, *refs):
    (hidden, down, first, second), sems = refs[:4], refs[4]
    slots = hidden.shape[0] // 2
    half = lax.axis_index("expert") // (lax.axis_size("expert") // 2)
    pairs = [(down_hbm, down), (first_hbm, first), (second_hbm, second)]
    for part in (0, 1):
        base = pl.multiple_of(jnp.bitwise_xor(half, part) * slots, slots)
        pairs.append((hidden_hbm.at[pl.ds(base, slots), :], hidden.at[pl.ds(slots * part, slots), :]))
    for copy in start_copies(pairs, sems):
        copy.wait()


def forward_kernel(
    hidden, down, first, second, low_one, low_two, out_one, out_two
):
    slots = out_one.shape[0]
    low = lax.dot_general(
        hidden[...], first[...], over_last, preferred_element_type=jnp.float32
    ).astype(jnp.bfloat16)
    low_one[...] = low[:slots]
    low_two[...] = low[slots:]
    for cut in pieces(out_one.shape[1], 512):
        values = jnp.dot(
            hidden[...], down[:, cut], preferred_element_type=jnp.float32
        ) + adapter_scale * jnp.dot(low, second[:, cut], preferred_element_type=jnp.float32)
        out_one[:, cut] = values[:slots]
        out_two[:, cut] = values[slots:]


def combine(me, capacity, blocks, out_ref, scaled_ref, pair_ref, base):
    count, tokens, width = len(blocks), blocks[0].shape[0], out_ref.shape[1]
    slots = count * capacity
    hits, weights = [], []
    for block in blocks:
        meta = block[0:16, width : width + lanes].astype(jnp.float32)
        match = meta[0:8] == me.astype(jnp.float32)
        hits.append(jnp.sum(jnp.where(match, 1.0, 0.0), axis=0, keepdims=True))
        weights.append(jnp.sum(jnp.where(match, meta[8:16], 0.0), axis=0, keepdims=True))
    hit = jnp.concatenate(hits, axis=0)
    weight = jnp.concatenate(weights, axis=0)
    before = (
        lax.broadcasted_iota(jnp.int32, (lanes, lanes), 0)
        < lax.broadcasted_iota(jnp.int32, (lanes, lanes), 1)
    )
    earlier = jnp.dot(
        hit.astype(jnp.bfloat16),
        jnp.where(before, 1.0, 0.0).astype(jnp.bfloat16),
        preferred_element_type=jnp.float32,
    )
    source = jnp.bitwise_xor(lax.broadcasted_iota(jnp.int32, (count, lanes), 0), me % count)
    target = jnp.where(hit > 0.0, (source * capacity).astype(jnp.float32) + earlier, -1.0)
    per = lanes // tokens
    lane = lax.broadcasted_iota(jnp.int32, (1, lanes), 1)
    slot = lax.broadcasted_iota(jnp.int32, (slots, lanes), 0).astype(jnp.float32)

    def merged(rows, q):
        row = rows[per * q : per * q + 1]
        for r in range(1, per):
            shifted = pltpu.roll(rows[per * q + r : per * q + r + 1], tokens * r, 1)
            row = jnp.where(lane >= tokens * r, shifted, row)
        return row

    picks, column = [], jnp.zeros((slots, 1), jnp.float32)
    for q in range(count // per):
        pick = jnp.where(slot == merged(target, q), 1.0, 0.0)
        column = column + jnp.sum(pick * merged(weight, q), axis=1, keepdims=True)
        picks.append(pick)
    picker = jnp.concatenate([pick.astype(jnp.bfloat16) for pick in picks], axis=1)
    grads = jnp.zeros((slots, 1), jnp.float32)
    for cut in pieces(width, 512):
        gathered_rows = jnp.concatenate([block[:, cut] for block in blocks], axis=0)
        rows = jnp.dot(picker, gathered_rows, preferred_element_type=jnp.float32)
        grads = grads + jnp.sum(rows * out_ref[:, cut], axis=1, keepdims=True)
        scaled_ref[:, cut] = (rows * column).astype(jnp.bfloat16)
    for q in range(count // per):
        row = jnp.sum(picks[q] * grads, axis=0, keepdims=True)
        for r in range(per):
            s = base + per * q + r
            pair_ref[s : s + 1, :] = row if r == 0 else pltpu.roll(row, lanes - tokens * r, 1)


def factor_sums(part, scaled_ref, low_ref, hidden_ref, second_ref):
    slots = scaled_ref.shape[0]
    scaled = scaled_ref[...]
    lowered = lax.dot_general(
        scaled, second_ref[...], over_last, preferred_element_type=jnp.float32
    ).astype(jnp.bfloat16)
    hidden = hidden_ref[slots * part : slots * (part + 1), :]
    first = lax.dot_general(lowered, hidden, over_first, preferred_element_type=jnp.float32)
    second = lax.dot_general(
        low_ref[...], scaled, over_first, preferred_element_type=jnp.float32
    )
    return lowered, adapter_scale * first, adapter_scale * second


def first_kernel(count, capacity, *refs):
    blocks, (out_ref, scaled_ref, pair_ref) = refs[:count], refs[count:]
    combine(lax.axis_index("expert"), capacity, blocks, out_ref, scaled_ref, pair_ref, 0)


def early_kernel(
    scaled_ref, low_ref, hidden_ref, second_ref, lowered_ref, dfirst_ref, dsecond_ref
):
    lowered_ref[...], dfirst_ref[...], dsecond_ref[...] = factor_sums(
        0, scaled_ref, low_ref, hidden_ref, second_ref
    )


def combine_kernel(count, capacity, *refs):
    blocks, (out_ref, before_ref, scaled_ref, pair_ref) = refs[:count], refs[count:]
    pair_ref[:count, :] = before_ref[...]
    combine(
        lax.axis_index("expert"), capacity, blocks, out_ref, scaled_ref, pair_ref, count
    )


def cotangent_of(scaled_ref, lowered, down_ref, first_ref):
    fixed = lax.dot_general(
        scaled_ref[...], down_ref[...], over_last, preferred_element_type=jnp.float32
    )
    adapter = jnp.dot(lowered, first_ref[...], preferred_element_type=jnp.float32)
    return (fixed + adapter_scale * adapter).astype(jnp.bfloat16)


def late_kernel(
    scaled_ref,
    low_ref,
    hidden_ref,
    down_ref,
    first_ref,
    second_ref,
    dfirst_before,
    dsecond_before,
    cot_ref,
    dfirst_ref,
    dsecond_ref,
):
    lowered, dfirst, dsecond = factor_sums(1, scaled_ref, low_ref, hidden_ref, second_ref)
    dfirst_ref[...] = dfirst + dfirst_before[...]
    dsecond_ref[...] = dsecond + dsecond_before[...]
    cot_ref[...] = cotangent_of(scaled_ref, lowered, down_ref, first_ref)


def cotangent_kernel(count, scaled_ref, lowered_ref, down_ref, first_ref, late_ref, cot_ref):
    half = lax.axis_index("expert") // count
    slots = scaled_ref.shape[0]
    here = pl.ds(pl.multiple_of(half * slots, slots), slots)
    there = pl.ds(pl.multiple_of((1 - half) * slots, slots), slots)
    cot_ref[there, :] = late_ref[...]
    cot_ref[here, :] = cotangent_of(scaled_ref, lowered_ref[...], down_ref, first_ref)


def gathered(
    output_cotangent,
    route,
    routing_weights,
    hidden,
    down_weight,
    first_adapter_factors,
    second_adapter_factors,
):
    _, _, sources, capacity, hidden_width = hidden.shape
    tokens, width = output_cotangent.shape
    rank = first_adapter_factors.shape[2]
    count = lax.axis_size("expert")
    slots = sources * capacity
    half = count // 2
    bf16, f32 = jnp.bfloat16, jnp.float32

    def swap(array, distance):
        return lax.ppermute(array, "expert", [(i, i ^ distance) for i in range(count)])

    def call(limit, kernel, outs, spaces, scratch, *operands, plain=()):
        return pl.pallas_call(
            kernel,
            out_shape=tuple(
                jax.ShapeDtypeStruct(*out) if i in plain else pltpu.VMEM(*out)
                for i, out in enumerate(outs)
            ),
            in_specs=[pl.BlockSpec(memory_space=space) for space in spaces],
            out_specs=(pl.BlockSpec(memory_space=pltpu.VMEM),) * len(outs),
            scratch_shapes=scratch,
            compiler_params=pltpu.CompilerParams(vmem_limit_bytes=limit * mebibyte),
            name=getattr(kernel, "func", kernel).__name__,
        )(*map(pltpu.with_memory_space_constraint, operands, spaces))

    route_rows = route.T
    payload, wanted = call(
        8,
        pack_kernel,
        [((tokens, width + lanes), bf16), (route_rows.shape, jnp.int32)],
        [pltpu.HBM] * 3,
        [
            pltpu.VMEM(route_rows.shape, jnp.int32),
            pltpu.VMEM(route_rows.shape, bf16),
            pltpu.SemaphoreType.DMA((3,)),
        ],
        output_cotangent,
        route_rows,
        routing_weights.T,
    )
    blocks = {0: payload}
    far = [d for d in range(4, count, 4)]
    near = [d for d in far if d < half]
    late = [d for d in far if d >= half]
    direct = [d for d in far if d & (d - 1) == 0]
    for d in direct[::-1]:
        blocks[d] = swap(payload, d)
    blocks[2] = swap(payload, 2)
    parameters = (
        hidden.reshape(slots, hidden_width),
        down_weight[0],
        first_adapter_factors[0].T,
        second_adapter_factors[0],
    )
    held = call(
        8,
        load_kernel,
        [(array.shape, bf16) for array in parameters],
        [pltpu.HBM] * 4,
        [pltpu.SemaphoreType.DMA((5,))],
        *parameters,
    )
    blocks[near[0]], held = lax.optimization_barrier((blocks[near[0]], held))
    low, low_late, out, out_late = call(
        24,
        forward_kernel,
        [((slots // 2, rank), bf16)] * 2 + [((slots // 2, width), f32)] * 2,
        [pltpu.VMEM] * 4,
        [],
        *held,
    )

    for d in far:
        if d not in direct:
            blocks[d] = swap(blocks[half], d - half)
    for d in far:
        blocks[d + 2] = swap(blocks[d], 2)
    for d in [0] + near:
        blocks[d + 1] = swap(blocks[d], 1)
        blocks[d + 3] = swap(blocks[d + 2], 1)
    hidden_held, down, first, second = held
    grads = [((rank, hidden_width), f32), ((rank, width), f32)]
    lowered = ((slots // 2, rank), bf16)
    scaled, pair = call(
        24,
        functools.partial(first_kernel, half, capacity),
        [((slots // 2, width), bf16), ((half, lanes), f32)],
        [pltpu.VMEM] * (half + 1),
        [],
        *[blocks[s] for s in range(half)],
        out,
    )
    d = late[-1] + 2
    blocks[d], scaled, pair = lax.optimization_barrier((blocks[d], scaled, pair))
    for d in late:
        blocks[d + 1] = swap(blocks[d], 1)
        blocks[d + 3] = swap(blocks[d + 2], 1)
    lowered_early, dfirst, dsecond = call(
        24,
        early_kernel,
        [lowered, *grads],
        [pltpu.VMEM] * 4,
        [],
        scaled,
        low,
        hidden_held,
        second,
    )
    out_late, dsecond = lax.optimization_barrier((out_late, dsecond))
    scaled_late, pair = call(
        24,
        functools.partial(combine_kernel, half, capacity),
        [((slots // 2, width), bf16), ((count, lanes), f32)],
        [pltpu.VMEM] * (half + 2),
        [],
        *[blocks[s] for s in range(half, count)],
        out_late,
        pair,
    )
    late_rows = ((slots // 2, hidden_width), bf16)
    cotangent, dfirst, dsecond = call(
        24,
        late_kernel,
        [late_rows, *grads],
        [pltpu.VMEM] * 8,
        [],
        scaled_late,
        low_late,
        *held,
        dfirst,
        dsecond,
        plain=(1, 2),
    )

    distance = lax.broadcasted_iota(jnp.int32, pair.shape, 0)
    order = far
    moved = [swap(pair, d) for d in order]
    for d, values in zip(order, moved):
        pair = jnp.where(distance - jnp.bitwise_and(distance, 3) == d, values, pair)
    pair, cotangent, dfirst, dsecond = lax.optimization_barrier(
        (pair, cotangent, dfirst, dsecond)
    )
    (cotangent,) = call(
        24,
        functools.partial(cotangent_kernel, half),
        [((slots, hidden_width), bf16)],
        [pltpu.VMEM] * 5,
        [],
        scaled,
        lowered_early,
        down,
        first,
        cotangent,
        plain=(0,),
    )
    moved = [swap(pair, d) for d in (1, 2, 3)]
    for d, values in zip((1, 2, 3), moved):
        pair = jnp.where(jnp.bitwise_and(distance, 3) == d, values, pair)
    hop = lax.broadcasted_iota(jnp.int32, (count, 1, 1), 0)
    gradient = jnp.sum(jnp.where(wanted[None] == hop, pair[:, None, :tokens], 0.0), axis=0)
    return (
        cotangent.reshape(hidden.shape),
        dfirst.T[None],
        dsecond[None],
        gradient.T,
    )


def local(output_cotangent, route, routing_weights, hidden, *parameters):
    resident, pairs, sources, capacity, hidden_width = hidden.shape
    count = lax.axis_size("expert")
    tokens, top = route.shape
    gather = (
        pairs * lax.axis_size("dp") == 1
        and resident == 1
        and sources == count
        and count & (count - 1) == 0
        and 16 <= count <= 256
        and lanes % tokens == 0
        and (count // 2) % (lanes // tokens) == 0
        and (count // 2 * capacity) % 16 == 0
        and output_cotangent.shape[1] % 512 == 0
        and hidden_width % 256 == 0
        and top == 8
        and 16 <= tokens <= 2 * capacity
    )
    form = gathered if gather else dispatched
    return form(output_cotangent, route, routing_weights, hidden, *parameters)


def solution(mesh):
    in_specs = (
        P(("groups", "expert", "dp"), None),
        P(("groups", "expert", "dp"), None),
        P(("groups", "expert", "dp"), None),
        P(("groups", "expert"), "dp", None, None, None),
        P("expert", "dp", None),
        P("expert", None, None),
        P("expert", None, None),
    )
    out_specs = (
        P(("groups", "expert"), "dp", None, None, None),
        P(("groups", "expert"), None, None),
        P(("groups", "expert"), None, None),
        P(("groups", "expert", "dp"), None),
    )
    return jax.shard_map(local, mesh=mesh, in_specs=in_specs, out_specs=out_specs, check_vma=False)
```

```python
import functools

import jax
import jax.numpy as jnp
from jax import lax
from jax.experimental import pallas as pl
from jax.experimental.pallas import tpu as pltpu
from jax.sharding import PartitionSpec as P

adapter_scale = 2.0
lanes = 128
mebibyte = 1 << 20
over_last = (((1,), (1,)), ((), ()))
over_first = (((0,), (0,)), ((), ()))


def slot_positions(route, expert_total):
    expert_ids = lax.broadcasted_iota(jnp.int32, (1, 1, expert_total), 2)
    expert_hits = jnp.sum((route[:, :, None] == expert_ids).astype(jnp.int32), axis=1)
    earlier = jnp.cumsum(expert_hits, axis=0) - expert_hits
    return jnp.take_along_axis(earlier, route, axis=1)


def dispatched(
    output_cotangent,
    route,
    routing_weights,
    hidden,
    down_weight,
    first_adapter_factors,
    second_adapter_factors,
):
    resident, pair_one, sources, capacity, hidden_width = hidden.shape
    expert_count = lax.axis_size("expert")
    expert_total = resident * expert_count
    model_width = output_cotangent.shape[1]
    position = slot_positions(route, expert_total)
    target = route * capacity + position
    slot_cells = lax.broadcasted_iota(jnp.int32, (expert_total * capacity, 1, 1), 0)
    matches = slot_cells == target[None, :, :]
    picker = jnp.any(matches, axis=2).astype(jnp.bfloat16)
    send_rows = jnp.dot(picker, output_cotangent, preferred_element_type=jnp.float32).astype(
        jnp.bfloat16
    )
    send_rows = send_rows.reshape(expert_total, capacity, model_width)
    send_weight = jnp.sum(
        jnp.where(matches, routing_weights[None, :, :].astype(jnp.float32), 0.0), axis=(1, 2)
    )
    send_weight = send_weight.astype(jnp.bfloat16).reshape(expert_total, capacity)
    recv_rows, recv_weight = (
        lax.all_to_all(send_rows, "expert", split_axis=0, concat_axis=0, tiled=True),
        lax.all_to_all(send_weight, "expert", split_axis=0, concat_axis=0, tiled=True),
    )
    grad_rows = recv_rows.reshape(sources, resident, capacity, model_width)
    scales = recv_weight.reshape(sources, resident, capacity)
    hidden_inputs = hidden.reshape(resident, sources, capacity, hidden_width)
    reduced_rank_product = jnp.einsum(
        "bwlv,bvs->bwls", hidden_inputs, first_adapter_factors, preferred_element_type=jnp.float32
    ).astype(jnp.bfloat16)
    adapter_result = jnp.einsum(
        "nvli,nit->vnlt",
        reduced_rank_product,
        second_adapter_factors,
        preferred_element_type=jnp.float32,
    )
    fixed_output = jnp.einsum(
        "ejcf,efd->jecd",
        hidden_inputs,
        lax.all_gather(down_weight, "dp", axis=1, tiled=True),
        preferred_element_type=jnp.float32,
    )
    output_values = fixed_output + adapter_scale * adapter_result
    slot_grad = jnp.sum(grad_rows.astype(jnp.float32) * output_values, axis=3)
    scaled_result = (scales[..., None].astype(jnp.float32) * grad_rows.astype(jnp.float32)).astype(
        jnp.bfloat16
    )
    projected_down = jnp.einsum(
        "mzxl,zil->mzxi", scaled_result, second_adapter_factors, preferred_element_type=jnp.float32
    ).astype(jnp.bfloat16)
    fixed_backward = jnp.einsum(
        "jecd,efd->ejcf",
        scaled_result,
        lax.all_gather(down_weight, "dp", axis=1, tiled=True),
        preferred_element_type=jnp.float32,
    )
    activation_cotangent = fixed_backward + adapter_scale * jnp.einsum(
        "mwsa,wqa->wmsq", projected_down, first_adapter_factors, preferred_element_type=jnp.float32
    )
    hidden_cotangent = activation_cotangent.astype(jnp.bfloat16).reshape(hidden.shape)
    first_share = adapter_scale * jnp.einsum(
        "ejcf,jecr->efr", hidden_inputs, projected_down, preferred_element_type=jnp.float32
    )
    second_share = adapter_scale * jnp.einsum(
        "ejcr,jecd->erd", reduced_rank_product, scaled_result, preferred_element_type=jnp.float32
    )
    first_factor_gradient, second_factor_gradient = lax.psum((first_share, second_share), "dp")
    returned_grads = lax.all_to_all(slot_grad, "expert", split_axis=0, concat_axis=0, tiled=True)
    returned_flat = returned_grads.reshape(expert_total * capacity)
    routing_weight_gradient = jnp.sum(jnp.where(matches, returned_flat[:, None, None], 0.0), axis=0)
    return (
        hidden_cotangent,
        first_factor_gradient,
        second_factor_gradient,
        routing_weight_gradient,
    )


def start_copies(pairs, sems):
    copies = [pltpu.make_async_copy(a, b, sems.at[i]) for i, (a, b) in enumerate(pairs)]
    for copy in copies:
        copy.start()
    return copies


def pack_kernel(
    cotangent_hbm, route_hbm, weight_hbm, payload_ref, wanted_ref, route_vmem, weight_vmem, sems
):
    tokens, width = cotangent_hbm.shape
    copies = start_copies(
        [
            (route_hbm, route_vmem),
            (weight_hbm, weight_vmem),
            (cotangent_hbm, payload_ref.at[:, pl.ds(0, width)]),
        ],
        sems,
    )
    payload_ref[:, width:] = jnp.full((tokens, lanes), -1.0, jnp.bfloat16)
    copies[0].wait()
    copies[1].wait()
    wanted_ref[...] = jnp.bitwise_xor(route_vmem[...], lax.axis_index("expert"))
    both = jnp.concatenate(
        [route_vmem[...].astype(jnp.float32), weight_vmem[...].astype(jnp.float32)], axis=0
    )
    payload_ref[:16, width : width + tokens] = both.astype(jnp.bfloat16)
    copies[2].wait()


def pieces(total, size):
    return [slice(start, start + size) for start in range(0, total, size)]


def load_kernel(hidden_hbm, down_hbm, first_hbm, second_hbm, *refs):
    (hidden, down, first, second), sems = refs[:4], refs[4]
    slots = hidden.shape[0] // 2
    half = lax.axis_index("expert") // (lax.axis_size("expert") // 2)
    pairs = [(down_hbm, down), (first_hbm, first), (second_hbm, second)]
    for part in (0, 1):
        base = pl.multiple_of(jnp.bitwise_xor(half, part) * slots, slots)
        pairs.append((hidden_hbm.at[pl.ds(base, slots), :], hidden.at[pl.ds(slots * part, slots), :]))
    for copy in start_copies(pairs, sems):
        copy.wait()


def forward_kernel(
    hidden, down, first, second, low_one, low_two, out_one, out_two
):
    slots = out_one.shape[0]
    low = lax.dot_general(
        hidden[...], first[...], over_last, preferred_element_type=jnp.float32
    ).astype(jnp.bfloat16)
    low_one[...] = low[:slots]
    low_two[...] = low[slots:]
    for cut in pieces(out_one.shape[1], 512):
        values = jnp.dot(
            hidden[...], down[:, cut], preferred_element_type=jnp.float32
        ) + adapter_scale * jnp.dot(low, second[:, cut], preferred_element_type=jnp.float32)
        out_one[:, cut] = values[:slots]
        out_two[:, cut] = values[slots:]


def combine(me, capacity, blocks, out_ref, scaled_ref, pair_ref, base):
    count, tokens, width = len(blocks), blocks[0].shape[0], out_ref.shape[1]
    slots = count * capacity
    hits, weights = [], []
    for block in blocks:
        meta = block[0:16, width : width + lanes].astype(jnp.float32)
        match = meta[0:8] == me.astype(jnp.float32)
        hits.append(jnp.sum(jnp.where(match, 1.0, 0.0), axis=0, keepdims=True))
        weights.append(jnp.sum(jnp.where(match, meta[8:16], 0.0), axis=0, keepdims=True))
    hit = jnp.concatenate(hits, axis=0)
    weight = jnp.concatenate(weights, axis=0)
    before = (
        lax.broadcasted_iota(jnp.int32, (lanes, lanes), 0)
        < lax.broadcasted_iota(jnp.int32, (lanes, lanes), 1)
    )
    earlier = jnp.dot(
        hit.astype(jnp.bfloat16),
        jnp.where(before, 1.0, 0.0).astype(jnp.bfloat16),
        preferred_element_type=jnp.float32,
    )
    source = jnp.bitwise_xor(lax.broadcasted_iota(jnp.int32, (count, lanes), 0), me % count)
    target = jnp.where(hit > 0.0, (source * capacity).astype(jnp.float32) + earlier, -1.0)
    per = lanes // tokens
    lane = lax.broadcasted_iota(jnp.int32, (1, lanes), 1)
    slot = lax.broadcasted_iota(jnp.int32, (slots, lanes), 0).astype(jnp.float32)

    def merged(rows, q):
        row = rows[per * q : per * q + 1]
        for r in range(1, per):
            shifted = pltpu.roll(rows[per * q + r : per * q + r + 1], tokens * r, 1)
            row = jnp.where(lane >= tokens * r, shifted, row)
        return row

    picks, column = [], jnp.zeros((slots, 1), jnp.float32)
    for q in range(count // per):
        pick = jnp.where(slot == merged(target, q), 1.0, 0.0)
        column = column + jnp.sum(pick * merged(weight, q), axis=1, keepdims=True)
        picks.append(pick)
    picker = jnp.concatenate([pick.astype(jnp.bfloat16) for pick in picks], axis=1)
    grads = jnp.zeros((slots, 1), jnp.float32)
    for cut in pieces(width, 512):
        gathered_rows = jnp.concatenate([block[:, cut] for block in blocks], axis=0)
        rows = jnp.dot(picker, gathered_rows, preferred_element_type=jnp.float32)
        grads = grads + jnp.sum(rows * out_ref[:, cut], axis=1, keepdims=True)
        scaled_ref[:, cut] = (rows * column).astype(jnp.bfloat16)
    for q in range(count // per):
        row = jnp.sum(picks[q] * grads, axis=0, keepdims=True)
        for r in range(per):
            s = base + per * q + r
            pair_ref[s : s + 1, :] = row if r == 0 else pltpu.roll(row, lanes - tokens * r, 1)


def factor_sums(part, scaled_ref, low_ref, hidden_ref, second_ref):
    slots = scaled_ref.shape[0]
    scaled = scaled_ref[...]
    lowered = lax.dot_general(
        scaled, second_ref[...], over_last, preferred_element_type=jnp.float32
    ).astype(jnp.bfloat16)
    hidden = hidden_ref[slots * part : slots * (part + 1), :]
    first = lax.dot_general(lowered, hidden, over_first, preferred_element_type=jnp.float32)
    second = lax.dot_general(
        low_ref[...], scaled, over_first, preferred_element_type=jnp.float32
    )
    return lowered, adapter_scale * first, adapter_scale * second


def first_kernel(count, capacity, *refs):
    blocks, (out_ref, scaled_ref, pair_ref) = refs[:count], refs[count:]
    combine(lax.axis_index("expert"), capacity, blocks, out_ref, scaled_ref, pair_ref, 0)


def early_kernel(
    scaled_ref, low_ref, hidden_ref, second_ref, lowered_ref, dfirst_ref, dsecond_ref
):
    lowered_ref[...], dfirst_ref[...], dsecond_ref[...] = factor_sums(
        0, scaled_ref, low_ref, hidden_ref, second_ref
    )


def combine_kernel(count, capacity, *refs):
    blocks, (out_ref, before_ref, scaled_ref, pair_ref) = refs[:count], refs[count:]
    pair_ref[:count, :] = before_ref[...]
    combine(
        lax.axis_index("expert"), capacity, blocks, out_ref, scaled_ref, pair_ref, count
    )


def cotangent_of(scaled_ref, lowered, down_ref, first_ref):
    fixed = lax.dot_general(
        scaled_ref[...], down_ref[...], over_last, preferred_element_type=jnp.float32
    )
    adapter = jnp.dot(lowered, first_ref[...], preferred_element_type=jnp.float32)
    return (fixed + adapter_scale * adapter).astype(jnp.bfloat16)


def late_kernel(
    scaled_ref,
    low_ref,
    hidden_ref,
    down_ref,
    first_ref,
    second_ref,
    dfirst_before,
    dsecond_before,
    cot_ref,
    dfirst_ref,
    dsecond_ref,
):
    lowered, dfirst, dsecond = factor_sums(1, scaled_ref, low_ref, hidden_ref, second_ref)
    dfirst_ref[...] = dfirst + dfirst_before[...]
    dsecond_ref[...] = dsecond + dsecond_before[...]
    cot_ref[...] = cotangent_of(scaled_ref, lowered, down_ref, first_ref)


def cotangent_kernel(count, scaled_ref, lowered_ref, down_ref, first_ref, late_ref, cot_ref):
    half = lax.axis_index("expert") // count
    slots = scaled_ref.shape[0]
    here = pl.ds(pl.multiple_of(half * slots, slots), slots)
    there = pl.ds(pl.multiple_of((1 - half) * slots, slots), slots)
    cot_ref[there, :] = late_ref[...]
    cot_ref[here, :] = cotangent_of(scaled_ref, lowered_ref[...], down_ref, first_ref)


def gathered(
    output_cotangent,
    route,
    routing_weights,
    hidden,
    down_weight,
    first_adapter_factors,
    second_adapter_factors,
):
    _, _, sources, capacity, hidden_width = hidden.shape
    tokens, width = output_cotangent.shape
    rank = first_adapter_factors.shape[2]
    count = lax.axis_size("expert")
    slots = sources * capacity
    half = count // 2
    bf16, f32 = jnp.bfloat16, jnp.float32

    def swap(array, distance):
        return lax.ppermute(array, "expert", [(i, i ^ distance) for i in range(count)])

    def call(limit, kernel, outs, spaces, scratch, *operands, plain=()):
        return pl.pallas_call(
            kernel,
            out_shape=tuple(
                jax.ShapeDtypeStruct(*out) if i in plain else pltpu.VMEM(*out)
                for i, out in enumerate(outs)
            ),
            in_specs=[pl.BlockSpec(memory_space=space) for space in spaces],
            out_specs=(pl.BlockSpec(memory_space=pltpu.VMEM),) * len(outs),
            scratch_shapes=scratch,
            compiler_params=pltpu.CompilerParams(vmem_limit_bytes=limit * mebibyte),
            name=getattr(kernel, "func", kernel).__name__,
        )(*map(pltpu.with_memory_space_constraint, operands, spaces))

    route_rows = route.T
    payload, wanted = call(
        8,
        pack_kernel,
        [((tokens, width + lanes), bf16), (route_rows.shape, jnp.int32)],
        [pltpu.HBM] * 3,
        [
            pltpu.VMEM(route_rows.shape, jnp.int32),
            pltpu.VMEM(route_rows.shape, bf16),
            pltpu.SemaphoreType.DMA((3,)),
        ],
        output_cotangent,
        route_rows,
        routing_weights.T,
    )
    blocks = {0: payload}
    far = [d for d in range(4, count, 4)]
    near = [d for d in far if d < half]
    late = [d for d in far if d >= half]
    direct = [d for d in far if d & (d - 1) == 0]
    for d in direct:
        blocks[d] = swap(payload, d)
    blocks[2] = swap(payload, 2)
    parameters = (
        hidden.reshape(slots, hidden_width),
        down_weight[0],
        first_adapter_factors[0].T,
        second_adapter_factors[0],
    )
    held = call(
        8,
        load_kernel,
        [(array.shape, bf16) for array in parameters],
        [pltpu.HBM] * 4,
        [pltpu.SemaphoreType.DMA((5,))],
        *parameters,
    )
    blocks[near[0]], held = lax.optimization_barrier((blocks[near[0]], held))
    low, low_late, out, out_late = call(
        24,
        forward_kernel,
        [((slots // 2, rank), bf16)] * 2 + [((slots // 2, width), f32)] * 2,
        [pltpu.VMEM] * 4,
        [],
        *held,
    )

    for d in far:
        if d not in direct:
            blocks[d] = swap(blocks[half], d - half)
    for d in far[::-1]:
        blocks[d + 2] = swap(blocks[d], 2)
    for d in [0] + near:
        blocks[d + 1] = swap(blocks[d], 1)
        blocks[d + 3] = swap(blocks[d + 2], 1)
    hidden_held, down, first, second = held
    grads = [((rank, hidden_width), f32), ((rank, width), f32)]
    lowered = ((slots // 2, rank), bf16)
    scaled, pair = call(
        24,
        functools.partial(first_kernel, half, capacity),
        [((slots // 2, width), bf16), ((half, lanes), f32)],
        [pltpu.VMEM] * (half + 1),
        [],
        *[blocks[s] for s in range(half)],
        out,
    )
    d = late[-1] + 2
    blocks[d], scaled, pair = lax.optimization_barrier((blocks[d], scaled, pair))
    for d in late:
        blocks[d + 1] = swap(blocks[d], 1)
        blocks[d + 3] = swap(blocks[d + 2], 1)
    lowered_early, dfirst, dsecond = call(
        24,
        early_kernel,
        [lowered, *grads],
        [pltpu.VMEM] * 4,
        [],
        scaled,
        low,
        hidden_held,
        second,
    )
    out_late, dsecond = lax.optimization_barrier((out_late, dsecond))
    scaled_late, pair = call(
        24,
        functools.partial(combine_kernel, half, capacity),
        [((slots // 2, width), bf16), ((count, lanes), f32)],
        [pltpu.VMEM] * (half + 2),
        [],
        *[blocks[s] for s in range(half, count)],
        out_late,
        pair,
    )
    late_rows = ((slots // 2, hidden_width), bf16)
    cotangent, dfirst, dsecond = call(
        24,
        late_kernel,
        [late_rows, *grads],
        [pltpu.VMEM] * 8,
        [],
        scaled_late,
        low_late,
        *held,
        dfirst,
        dsecond,
        plain=(1, 2),
    )

    distance = lax.broadcasted_iota(jnp.int32, pair.shape, 0)
    order = far
    moved = [swap(pair, d) for d in order]
    for d, values in zip(order, moved):
        pair = jnp.where(distance - jnp.bitwise_and(distance, 3) == d, values, pair)
    pair, cotangent, dfirst, dsecond = lax.optimization_barrier(
        (pair, cotangent, dfirst, dsecond)
    )
    (cotangent,) = call(
        24,
        functools.partial(cotangent_kernel, half),
        [((slots, hidden_width), bf16)],
        [pltpu.VMEM] * 5,
        [],
        scaled,
        lowered_early,
        down,
        first,
        cotangent,
        plain=(0,),
    )
    moved = [swap(pair, d) for d in (1, 2, 3)]
    for d, values in zip((1, 2, 3), moved):
        pair = jnp.where(jnp.bitwise_and(distance, 3) == d, values, pair)
    hop = lax.broadcasted_iota(jnp.int32, (count, 1, 1), 0)
    gradient = jnp.sum(jnp.where(wanted[None] == hop, pair[:, None, :tokens], 0.0), axis=0)
    return (
        cotangent.reshape(hidden.shape),
        dfirst.T[None],
        dsecond[None],
        gradient.T,
    )


def local(output_cotangent, route, routing_weights, hidden, *parameters):
    resident, pairs, sources, capacity, hidden_width = hidden.shape
    count = lax.axis_size("expert")
    tokens, top = route.shape
    gather = (
        pairs * lax.axis_size("dp") == 1
        and resident == 1
        and sources == count
        and count & (count - 1) == 0
        and 16 <= count <= 256
        and lanes % tokens == 0
        and (count // 2) % (lanes // tokens) == 0
        and (count // 2 * capacity) % 16 == 0
        and output_cotangent.shape[1] % 512 == 0
        and hidden_width % 256 == 0
        and top == 8
        and 16 <= tokens <= 2 * capacity
    )
    form = gathered if gather else dispatched
    return form(output_cotangent, route, routing_weights, hidden, *parameters)


def solution(mesh):
    in_specs = (
        P(("groups", "expert", "dp"), None),
        P(("groups", "expert", "dp"), None),
        P(("groups", "expert", "dp"), None),
        P(("groups", "expert"), "dp", None, None, None),
        P("expert", "dp", None),
        P("expert", None, None),
        P("expert", None, None),
    )
    out_specs = (
        P(("groups", "expert"), "dp", None, None, None),
        P(("groups", "expert"), None, None),
        P(("groups", "expert"), None, None),
        P(("groups", "expert", "dp"), None),
    )
    return jax.shard_map(local, mesh=mesh, in_specs=in_specs, out_specs=out_specs, check_vma=False)
```

```python
import functools

import jax
import jax.numpy as jnp
from jax import lax
from jax.experimental import pallas as pl
from jax.experimental.pallas import tpu as pltpu
from jax.sharding import PartitionSpec as P

adapter_scale = 2.0
lanes = 128
mebibyte = 1 << 20
over_last = (((1,), (1,)), ((), ()))
over_first = (((0,), (0,)), ((), ()))


def slot_positions(route, expert_total):
    expert_ids = lax.broadcasted_iota(jnp.int32, (1, 1, expert_total), 2)
    expert_hits = jnp.sum((route[:, :, None] == expert_ids).astype(jnp.int32), axis=1)
    earlier = jnp.cumsum(expert_hits, axis=0) - expert_hits
    return jnp.take_along_axis(earlier, route, axis=1)


def dispatched(
    output_cotangent,
    route,
    routing_weights,
    hidden,
    down_weight,
    first_adapter_factors,
    second_adapter_factors,
):
    resident, pair_one, sources, capacity, hidden_width = hidden.shape
    expert_count = lax.axis_size("expert")
    expert_total = resident * expert_count
    model_width = output_cotangent.shape[1]
    position = slot_positions(route, expert_total)
    target = route * capacity + position
    slot_cells = lax.broadcasted_iota(jnp.int32, (expert_total * capacity, 1, 1), 0)
    matches = slot_cells == target[None, :, :]
    picker = jnp.any(matches, axis=2).astype(jnp.bfloat16)
    send_rows = jnp.dot(picker, output_cotangent, preferred_element_type=jnp.float32).astype(
        jnp.bfloat16
    )
    send_rows = send_rows.reshape(expert_total, capacity, model_width)
    send_weight = jnp.sum(
        jnp.where(matches, routing_weights[None, :, :].astype(jnp.float32), 0.0), axis=(1, 2)
    )
    send_weight = send_weight.astype(jnp.bfloat16).reshape(expert_total, capacity)
    recv_rows, recv_weight = (
        lax.all_to_all(send_rows, "expert", split_axis=0, concat_axis=0, tiled=True),
        lax.all_to_all(send_weight, "expert", split_axis=0, concat_axis=0, tiled=True),
    )
    grad_rows = recv_rows.reshape(sources, resident, capacity, model_width)
    scales = recv_weight.reshape(sources, resident, capacity)
    hidden_inputs = hidden.reshape(resident, sources, capacity, hidden_width)
    reduced_rank_product = jnp.einsum(
        "bwlv,bvs->bwls", hidden_inputs, first_adapter_factors, preferred_element_type=jnp.float32
    ).astype(jnp.bfloat16)
    adapter_result = jnp.einsum(
        "nvli,nit->vnlt",
        reduced_rank_product,
        second_adapter_factors,
        preferred_element_type=jnp.float32,
    )
    fixed_output = jnp.einsum(
        "ejcf,efd->jecd",
        hidden_inputs,
        lax.all_gather(down_weight, "dp", axis=1, tiled=True),
        preferred_element_type=jnp.float32,
    )
    output_values = fixed_output + adapter_scale * adapter_result
    slot_grad = jnp.sum(grad_rows.astype(jnp.float32) * output_values, axis=3)
    scaled_result = (scales[..., None].astype(jnp.float32) * grad_rows.astype(jnp.float32)).astype(
        jnp.bfloat16
    )
    projected_down = jnp.einsum(
        "mzxl,zil->mzxi", scaled_result, second_adapter_factors, preferred_element_type=jnp.float32
    ).astype(jnp.bfloat16)
    fixed_backward = jnp.einsum(
        "jecd,efd->ejcf",
        scaled_result,
        lax.all_gather(down_weight, "dp", axis=1, tiled=True),
        preferred_element_type=jnp.float32,
    )
    activation_cotangent = fixed_backward + adapter_scale * jnp.einsum(
        "mwsa,wqa->wmsq", projected_down, first_adapter_factors, preferred_element_type=jnp.float32
    )
    hidden_cotangent = activation_cotangent.astype(jnp.bfloat16).reshape(hidden.shape)
    first_share = adapter_scale * jnp.einsum(
        "ejcf,jecr->efr", hidden_inputs, projected_down, preferred_element_type=jnp.float32
    )
    second_share = adapter_scale * jnp.einsum(
        "ejcr,jecd->erd", reduced_rank_product, scaled_result, preferred_element_type=jnp.float32
    )
    first_factor_gradient, second_factor_gradient = lax.psum((first_share, second_share), "dp")
    returned_grads = lax.all_to_all(slot_grad, "expert", split_axis=0, concat_axis=0, tiled=True)
    returned_flat = returned_grads.reshape(expert_total * capacity)
    routing_weight_gradient = jnp.sum(jnp.where(matches, returned_flat[:, None, None], 0.0), axis=0)
    return (
        hidden_cotangent,
        first_factor_gradient,
        second_factor_gradient,
        routing_weight_gradient,
    )


def start_copies(pairs, sems):
    copies = [pltpu.make_async_copy(a, b, sems.at[i]) for i, (a, b) in enumerate(pairs)]
    for copy in copies:
        copy.start()
    return copies


def pack_kernel(
    cotangent_hbm, route_hbm, weight_hbm, payload_ref, wanted_ref, route_vmem, weight_vmem, sems
):
    tokens, width = cotangent_hbm.shape
    copies = start_copies(
        [
            (route_hbm, route_vmem),
            (weight_hbm, weight_vmem),
            (cotangent_hbm, payload_ref.at[:, pl.ds(0, width)]),
        ],
        sems,
    )
    payload_ref[:, width:] = jnp.full((tokens, lanes), -1.0, jnp.bfloat16)
    copies[0].wait()
    copies[1].wait()
    wanted_ref[...] = jnp.bitwise_xor(route_vmem[...], lax.axis_index("expert"))
    both = jnp.concatenate(
        [route_vmem[...].astype(jnp.float32), weight_vmem[...].astype(jnp.float32)], axis=0
    )
    payload_ref[:16, width : width + tokens] = both.astype(jnp.bfloat16)
    copies[2].wait()


def pieces(total, size):
    return [slice(start, start + size) for start in range(0, total, size)]


def load_kernel(hidden_hbm, down_hbm, first_hbm, second_hbm, *refs):
    (hidden, down, first, second), sems = refs[:4], refs[4]
    slots = hidden.shape[0] // 2
    half = lax.axis_index("expert") // (lax.axis_size("expert") // 2)
    pairs = [(down_hbm, down), (first_hbm, first), (second_hbm, second)]
    for part in (0, 1):
        base = pl.multiple_of(jnp.bitwise_xor(half, part) * slots, slots)
        pairs.append((hidden_hbm.at[pl.ds(base, slots), :], hidden.at[pl.ds(slots * part, slots), :]))
    for copy in start_copies(pairs, sems):
        copy.wait()


def forward_kernel(
    hidden, down, first, second, low_one, low_two, out_one, out_two
):
    slots = out_one.shape[0]
    low = lax.dot_general(
        hidden[...], first[...], over_last, preferred_element_type=jnp.float32
    ).astype(jnp.bfloat16)
    low_one[...] = low[:slots]
    low_two[...] = low[slots:]
    for cut in pieces(out_one.shape[1], 512):
        values = jnp.dot(
            hidden[...], down[:, cut], preferred_element_type=jnp.float32
        ) + adapter_scale * jnp.dot(low, second[:, cut], preferred_element_type=jnp.float32)
        out_one[:, cut] = values[:slots]
        out_two[:, cut] = values[slots:]


def combine(me, capacity, blocks, out_ref, scaled_ref, pair_ref, base):
    count, tokens, width = len(blocks), blocks[0].shape[0], out_ref.shape[1]
    slots = count * capacity
    hits, weights = [], []
    for block in blocks:
        meta = block[0:16, width : width + lanes].astype(jnp.float32)
        match = meta[0:8] == me.astype(jnp.float32)
        hits.append(jnp.sum(jnp.where(match, 1.0, 0.0), axis=0, keepdims=True))
        weights.append(jnp.sum(jnp.where(match, meta[8:16], 0.0), axis=0, keepdims=True))
    hit = jnp.concatenate(hits, axis=0)
    weight = jnp.concatenate(weights, axis=0)
    before = (
        lax.broadcasted_iota(jnp.int32, (lanes, lanes), 0)
        < lax.broadcasted_iota(jnp.int32, (lanes, lanes), 1)
    )
    earlier = jnp.dot(
        hit.astype(jnp.bfloat16),
        jnp.where(before, 1.0, 0.0).astype(jnp.bfloat16),
        preferred_element_type=jnp.float32,
    )
    source = jnp.bitwise_xor(lax.broadcasted_iota(jnp.int32, (count, lanes), 0), me % count)
    target = jnp.where(hit > 0.0, (source * capacity).astype(jnp.float32) + earlier, -1.0)
    per = lanes // tokens
    lane = lax.broadcasted_iota(jnp.int32, (1, lanes), 1)
    slot = lax.broadcasted_iota(jnp.int32, (slots, lanes), 0).astype(jnp.float32)

    def merged(rows, q):
        row = rows[per * q : per * q + 1]
        for r in range(1, per):
            shifted = pltpu.roll(rows[per * q + r : per * q + r + 1], tokens * r, 1)
            row = jnp.where(lane >= tokens * r, shifted, row)
        return row

    picks, column = [], jnp.zeros((slots, 1), jnp.float32)
    for q in range(count // per):
        pick = jnp.where(slot == merged(target, q), 1.0, 0.0)
        column = column + jnp.sum(pick * merged(weight, q), axis=1, keepdims=True)
        picks.append(pick)
    picker = jnp.concatenate([pick.astype(jnp.bfloat16) for pick in picks], axis=1)
    grads = jnp.zeros((slots, 1), jnp.float32)
    for cut in pieces(width, 256):
        gathered_rows = jnp.concatenate([block[:, cut] for block in blocks], axis=0)
        rows = jnp.dot(picker, gathered_rows, preferred_element_type=jnp.float32)
        grads = grads + jnp.sum(rows * out_ref[:, cut], axis=1, keepdims=True)
        scaled_ref[:, cut] = (rows * column).astype(jnp.bfloat16)
    for q in range(count // per):
        row = jnp.sum(picks[q] * grads, axis=0, keepdims=True)
        for r in range(per):
            s = base + per * q + r
            pair_ref[s : s + 1, :] = row if r == 0 else pltpu.roll(row, lanes - tokens * r, 1)


def factor_sums(part, scaled_ref, low_ref, hidden_ref, second_ref):
    slots = scaled_ref.shape[0]
    scaled = scaled_ref[...]
    lowered = lax.dot_general(
        scaled, second_ref[...], over_last, preferred_element_type=jnp.float32
    ).astype(jnp.bfloat16)
    hidden = hidden_ref[slots * part : slots * (part + 1), :]
    first = lax.dot_general(lowered, hidden, over_first, preferred_element_type=jnp.float32)
    second = lax.dot_general(
        low_ref[...], scaled, over_first, preferred_element_type=jnp.float32
    )
    return lowered, adapter_scale * first, adapter_scale * second


def first_kernel(count, capacity, *refs):
    blocks, (out_ref, scaled_ref, pair_ref) = refs[:count], refs[count:]
    combine(lax.axis_index("expert"), capacity, blocks, out_ref, scaled_ref, pair_ref, 0)


def early_kernel(
    scaled_ref, low_ref, hidden_ref, second_ref, lowered_ref, dfirst_ref, dsecond_ref
):
    lowered_ref[...], dfirst_ref[...], dsecond_ref[...] = factor_sums(
        0, scaled_ref, low_ref, hidden_ref, second_ref
    )


def combine_kernel(count, capacity, *refs):
    blocks, (out_ref, before_ref, scaled_ref, pair_ref) = refs[:count], refs[count:]
    pair_ref[:count, :] = before_ref[...]
    combine(
        lax.axis_index("expert"), capacity, blocks, out_ref, scaled_ref, pair_ref, count
    )


def cotangent_of(scaled_ref, lowered, down_ref, first_ref):
    fixed = lax.dot_general(
        scaled_ref[...], down_ref[...], over_last, preferred_element_type=jnp.float32
    )
    adapter = jnp.dot(lowered, first_ref[...], preferred_element_type=jnp.float32)
    return (fixed + adapter_scale * adapter).astype(jnp.bfloat16)


def late_kernel(
    scaled_ref,
    low_ref,
    hidden_ref,
    down_ref,
    first_ref,
    second_ref,
    dfirst_before,
    dsecond_before,
    cot_ref,
    dfirst_ref,
    dsecond_ref,
):
    lowered, dfirst, dsecond = factor_sums(1, scaled_ref, low_ref, hidden_ref, second_ref)
    dfirst_ref[...] = dfirst + dfirst_before[...]
    dsecond_ref[...] = dsecond + dsecond_before[...]
    cot_ref[...] = cotangent_of(scaled_ref, lowered, down_ref, first_ref)


def cotangent_kernel(count, scaled_ref, lowered_ref, down_ref, first_ref, late_ref, cot_ref):
    half = lax.axis_index("expert") // count
    slots = scaled_ref.shape[0]
    here = pl.ds(pl.multiple_of(half * slots, slots), slots)
    there = pl.ds(pl.multiple_of((1 - half) * slots, slots), slots)
    cot_ref[there, :] = late_ref[...]
    cot_ref[here, :] = cotangent_of(scaled_ref, lowered_ref[...], down_ref, first_ref)


def gathered(
    output_cotangent,
    route,
    routing_weights,
    hidden,
    down_weight,
    first_adapter_factors,
    second_adapter_factors,
):
    _, _, sources, capacity, hidden_width = hidden.shape
    tokens, width = output_cotangent.shape
    rank = first_adapter_factors.shape[2]
    count = lax.axis_size("expert")
    slots = sources * capacity
    half = count // 2
    bf16, f32 = jnp.bfloat16, jnp.float32

    def swap(array, distance):
        return lax.ppermute(array, "expert", [(i, i ^ distance) for i in range(count)])

    def call(limit, kernel, outs, spaces, scratch, *operands, plain=()):
        return pl.pallas_call(
            kernel,
            out_shape=tuple(
                jax.ShapeDtypeStruct(*out) if i in plain else pltpu.VMEM(*out)
                for i, out in enumerate(outs)
            ),
            in_specs=[pl.BlockSpec(memory_space=space) for space in spaces],
            out_specs=(pl.BlockSpec(memory_space=pltpu.VMEM),) * len(outs),
            scratch_shapes=scratch,
            compiler_params=pltpu.CompilerParams(vmem_limit_bytes=limit * mebibyte),
            name=getattr(kernel, "func", kernel).__name__,
        )(*map(pltpu.with_memory_space_constraint, operands, spaces))

    route_rows = route.T
    payload, wanted = call(
        8,
        pack_kernel,
        [((tokens, width + lanes), bf16), (route_rows.shape, jnp.int32)],
        [pltpu.HBM] * 3,
        [
            pltpu.VMEM(route_rows.shape, jnp.int32),
            pltpu.VMEM(route_rows.shape, bf16),
            pltpu.SemaphoreType.DMA((3,)),
        ],
        output_cotangent,
        route_rows,
        routing_weights.T,
    )
    blocks = {0: payload}
    far = [d for d in range(4, count, 4)]
    near = [d for d in far if d < half]
    late = [d for d in far if d >= half]
    direct = [d for d in far if d & (d - 1) == 0]
    for d in direct[::-1]:
        blocks[d] = swap(payload, d)
    blocks[2] = swap(payload, 2)
    parameters = (
        hidden.reshape(slots, hidden_width),
        down_weight[0],
        first_adapter_factors[0].T,
        second_adapter_factors[0],
    )
    held = call(
        8,
        load_kernel,
        [(array.shape, bf16) for array in parameters],
        [pltpu.HBM] * 4,
        [pltpu.SemaphoreType.DMA((5,))],
        *parameters,
    )
    blocks[near[0]], held = lax.optimization_barrier((blocks[near[0]], held))
    low, low_late, out, out_late = call(
        24,
        forward_kernel,
        [((slots // 2, rank), bf16)] * 2 + [((slots // 2, width), f32)] * 2,
        [pltpu.VMEM] * 4,
        [],
        *held,
    )

    for d in far:
        if d not in direct:
            blocks[d] = swap(blocks[half], d - half)
    for d in far:
        blocks[d + 2] = swap(blocks[d], 2)
    for d in [0] + near:
        blocks[d + 1] = swap(blocks[d], 1)
        blocks[d + 3] = swap(blocks[d + 2], 1)
    hidden_held, down, first, second = held
    grads = [((rank, hidden_width), f32), ((rank, width), f32)]
    lowered = ((slots // 2, rank), bf16)
    scaled, pair = call(
        24,
        functools.partial(first_kernel, half, capacity),
        [((slots // 2, width), bf16), ((half, lanes), f32)],
        [pltpu.VMEM] * (half + 1),
        [],
        *[blocks[s] for s in range(half)],
        out,
    )
    d = late[-1] + 2
    blocks[d], scaled, pair = lax.optimization_barrier((blocks[d], scaled, pair))
    for d in late:
        blocks[d + 1] = swap(blocks[d], 1)
        blocks[d + 3] = swap(blocks[d + 2], 1)
    lowered_early, dfirst, dsecond = call(
        24,
        early_kernel,
        [lowered, *grads],
        [pltpu.VMEM] * 4,
        [],
        scaled,
        low,
        hidden_held,
        second,
    )
    out_late, dsecond = lax.optimization_barrier((out_late, dsecond))
    scaled_late, pair = call(
        24,
        functools.partial(combine_kernel, half, capacity),
        [((slots // 2, width), bf16), ((count, lanes), f32)],
        [pltpu.VMEM] * (half + 2),
        [],
        *[blocks[s] for s in range(half, count)],
        out_late,
        pair,
    )
    late_rows = ((slots // 2, hidden_width), bf16)
    cotangent, dfirst, dsecond = call(
        24,
        late_kernel,
        [late_rows, *grads],
        [pltpu.VMEM] * 8,
        [],
        scaled_late,
        low_late,
        *held,
        dfirst,
        dsecond,
        plain=(1, 2),
    )

    distance = lax.broadcasted_iota(jnp.int32, pair.shape, 0)
    order = far
    moved = [swap(pair, d) for d in order]
    for d, values in zip(order, moved):
        pair = jnp.where(distance - jnp.bitwise_and(distance, 3) == d, values, pair)
    pair, cotangent, dfirst, dsecond = lax.optimization_barrier(
        (pair, cotangent, dfirst, dsecond)
    )
    (cotangent,) = call(
        24,
        functools.partial(cotangent_kernel, half),
        [((slots, hidden_width), bf16)],
        [pltpu.VMEM] * 5,
        [],
        scaled,
        lowered_early,
        down,
        first,
        cotangent,
        plain=(0,),
    )
    moved = [swap(pair, d) for d in (1, 2, 3)]
    for d, values in zip((1, 2, 3), moved):
        pair = jnp.where(jnp.bitwise_and(distance, 3) == d, values, pair)
    hop = lax.broadcasted_iota(jnp.int32, (count, 1, 1), 0)
    gradient = jnp.sum(jnp.where(wanted[None] == hop, pair[:, None, :tokens], 0.0), axis=0)
    return (
        cotangent.reshape(hidden.shape),
        dfirst.T[None],
        dsecond[None],
        gradient.T,
    )


def local(output_cotangent, route, routing_weights, hidden, *parameters):
    resident, pairs, sources, capacity, hidden_width = hidden.shape
    count = lax.axis_size("expert")
    tokens, top = route.shape
    gather = (
        pairs * lax.axis_size("dp") == 1
        and resident == 1
        and sources == count
        and count & (count - 1) == 0
        and 16 <= count <= 256
        and lanes % tokens == 0
        and (count // 2) % (lanes // tokens) == 0
        and (count // 2 * capacity) % 16 == 0
        and output_cotangent.shape[1] % 512 == 0
        and hidden_width % 256 == 0
        and top == 8
        and 16 <= tokens <= 2 * capacity
    )
    form = gathered if gather else dispatched
    return form(output_cotangent, route, routing_weights, hidden, *parameters)


def solution(mesh):
    in_specs = (
        P(("groups", "expert", "dp"), None),
        P(("groups", "expert", "dp"), None),
        P(("groups", "expert", "dp"), None),
        P(("groups", "expert"), "dp", None, None, None),
        P("expert", "dp", None),
        P("expert", None, None),
        P("expert", None, None),
    )
    out_specs = (
        P(("groups", "expert"), "dp", None, None, None),
        P(("groups", "expert"), None, None),
        P(("groups", "expert"), None, None),
        P(("groups", "expert", "dp"), None),
    )
    return jax.shard_map(local, mesh=mesh, in_specs=in_specs, out_specs=out_specs, check_vma=False)
```
